512 devices in a mesh: row: 32 (over x_hi, z, core), col: 16 (over x_lo, y).
Axes of the slice: x: 4 (x_hi: 2, x_lo: 2; x = x_hi * 2 + x_lo), y: 8, z: 8, core: 2. Of those that a mesh axis runs over, the one named last changes fastest.
Arguments:
- pair: bfloat16 [512, 512, 128], P('row', 'col'), may hold values from -6 to 6
- pair_mask: int32 [512, 512], P('row', 'col'), may hold values 0 or 1
- in_weights: bfloat16 [128, 512], replicated, may hold values from -0.5 to 0.5
- gate_weight: bfloat16 [128, 128], replicated, may hold values from -0.5 to 0.5
- out_weight: bfloat16 [128, 128], replicated, may hold values from -0.5 to 0.5
Outputs:
- update: bfloat16 [512, 512, 128], P('row', 'col')
The draws below stay inside these ranges and needn't reach their ends.
All inputs are finite; a program needn't handle non-finite values. No bound on the sum of `pair_mask` on one device may be relied on, other than what follows from the above.
Results may differ from the reference program's by a relative error of at most 0.0078.
Values may be sent and summed in bfloat16 or wider, within the bound.
A program may use at most 64 MiB of HBM per device.

```python
import jax
import jax.numpy as jnp
from jax import lax

C = 128
CH = 128
N = 512


def set_ends(result, rng, smallest, largest):
    longest = result.shape.index(max(result.shape))
    spots = []
    for shift in (0, 1):
        where = [jax.random.randint(jax.random.fold_in(rng, axis), (), 0, length) for axis, length in enumerate(result.shape)]
        where[longest] = (where[longest] + shift) % result.shape[longest]
        spots.append(tuple(where))
    return result.at[spots[0]].set(smallest).at[spots[1]].set(largest)


def block_levels(stream_key, extent, pieces, low, top_value):
    gain = 1.0
    for position, parts in pieces:
        draws = jax.random.uniform(jax.random.fold_in(jax.random.fold_in(stream_key, 6), position), (parts,), jnp.float32, low / len(pieces), top_value / len(pieces))
        gain = gain * jnp.repeat(jnp.exp(draws), extent[position] // parts).reshape((-1,) + (1,) * (len(extent) - 1 - position))
    return gain


def bell_draw(key, dims, scale, most, cuts=(), kind=jnp.bfloat16):
    result = scale * jax.random.normal(key, dims, jnp.float32)
    if cuts:
        result = result * block_levels(key, dims, cuts, -0.22, 0.18)
    return jnp.clip(result, -most, most).astype(kind)


def setup_inputs(seed: int = 0) -> dict:
    key_of = jax.random.split(jax.random.key(seed), 6)
    return {
        "pair": bell_draw(key_of[0], (N, N, C), 1.0, 6.0, ((0, 32), (1, 16))),
        "pair_mask": set_ends((jax.random.randint(key_of[1], (N, N), 0, 8) < 7).astype(jnp.int32), jax.random.fold_in(key_of[1], 1), 0, 1),
        "in_weights": bell_draw(key_of[2], (C, 4 * CH), C ** -0.5, 0.5),
        "gate_weight": bell_draw(key_of[3], (C, C), C ** -0.5, 0.5),
        "out_weight": bell_draw(key_of[4], (CH, C), CH ** -0.5, 0.5),
    }


def layer_norm(values):
    mean = lax.optimization_barrier(jnp.mean(values, axis=-1, keepdims=True))
    centred = values - mean
    var = lax.optimization_barrier(jnp.mean(centred * centred, axis=-1, keepdims=True))
    return centred * jax.lax.rsqrt(var + 1e-05)

def reference(pair, pair_mask, in_weights, gate_weight, out_weight):
    count = pair.shape[0]
    width = pair.shape[2]
    hidden = in_weights.shape[1] // 4
    normed = layer_norm(pair.astype(jnp.float32).reshape(-1, width)).astype(jnp.bfloat16)
    proj = jnp.dot(normed, in_weights, preferred_element_type=jnp.float32)
    maskf = pair_mask.reshape(-1, 1).astype(jnp.float32)
    left = (maskf * jax.nn.sigmoid(proj[:, hidden:2 * hidden]) * proj[:, :hidden]).astype(jnp.bfloat16)
    right = (maskf * jax.nn.sigmoid(proj[:, 3 * hidden:]) * proj[:, 2 * hidden:3 * hidden]).astype(jnp.bfloat16)
    left = left.reshape(count, count, hidden).astype(jnp.float32)
    right = right.reshape(count, count, hidden).astype(jnp.float32)
    tri = jnp.einsum('ikc,jkc->ijc', left, right)
    tnorm = layer_norm(tri.reshape(-1, hidden)).astype(jnp.bfloat16)
    gate = jax.nn.sigmoid(jnp.dot(normed, gate_weight, preferred_element_type=jnp.float32))
    update = gate * jnp.dot(tnorm, out_weight, preferred_element_type=jnp.float32)
    return update.astype(jnp.bfloat16).reshape(count, count, width)
```

```python
import jax
import jax.numpy as jnp
from jax import lax
from jax.experimental import pallas as pl
from jax.experimental.pallas import tpu as pltpu
from jax.sharding import PartitionSpec as P

MESH = pl.DeviceIdType.MESH
F32 = jnp.float32
BF16 = jnp.bfloat16

ROWS, COLS = 32, 16
NZ = 8
IL, KL = 16, 32
N = 512
POS = IL * KL
C = 128


def layer_norm(values, axis):
    mean = jnp.mean(values, axis=axis, keepdims=True)
    centred = values - mean
    var = jnp.mean(centred * centred, axis=axis, keepdims=True)
    return centred * lax.rsqrt(var + 1e-05)


def sigmoid(x):
    return 0.5 * jnp.tanh(0.5 * x) + 0.5


def swap_blocks(v):
    lane = lax.broadcasted_iota(jnp.int32, v[0].shape, 1)
    low64 = lane < 64
    low32 = (lane % 64) < 32
    a = [None] * 4
    for c in range(2):
        a[c] = jnp.where(low64, v[c], pltpu.roll(v[c + 2], 64, 1))
        a[c + 2] = jnp.where(low64, pltpu.roll(v[c], 64, 1), v[c + 2])
    out = [None] * 4
    for h in (0, 2):
        out[h] = jnp.where(low32, a[h], pltpu.roll(a[h + 1], 32, 1))
        out[h + 1] = jnp.where(low32, pltpu.roll(a[h], 96, 1), a[h + 1])
    return out


def kernel(
    pair_hbm, mask_hbm, w_hbm, gw_hbm, ow_hbm, out_ref,
    pair_ref, mask_ref, w_ref, gw_ref, ow_ref,
    proj, gate, send1, recv1, turn, send2, recv_l, recv_r, send3, recv3, wide3, send4, recv4,
    load_sem, s1, r1, s2, r2l, r2r, s3, r3, s4, r4,
):
    r, c = lax.axis_index("row"), lax.axis_index("col")
    xh, z, core = r // 16, (r // 2) % NZ, r % 2
    zc = r % 16

    loads = []
    for n, (src, dst) in enumerate(
        ((pair_hbm, pair_ref), (mask_hbm, mask_ref), (w_hbm, w_ref), (gw_hbm, gw_ref), (ow_hbm, ow_ref))
    ):
        loads.append(pltpu.make_async_copy(src, dst, load_sem.at[n]))
        loads[-1].start()

    barrier = pltpu.get_barrier_semaphore()

    @pl.loop(1, COLS)
    def _(d):
        pl.semaphore_signal(barrier, inc=1, device_id=(r, (c + d) % COLS), device_id_type=MESH)

    @pl.loop(1, ROWS)
    def _(d):
        pl.semaphore_signal(barrier, inc=1, device_id=((r + d) % ROWS, c), device_id_type=MESH)

    for load in loads:
        load.wait()

    normed = layer_norm(pair_ref[...].reshape(POS, C).astype(F32), 1)
    eye = lax.broadcasted_iota(jnp.int32, (KL, KL), 0) == lax.broadcasted_iota(jnp.int32, (KL, KL), 1)
    maskf = mask_ref[...].astype(F32)
    column = jnp.concatenate(
        [jnp.sum(jnp.where(eye, maskf[il : il + 1, :], 0.0), axis=1, keepdims=True) for il in range(IL)], axis=0
    )
    masked = (normed * column).astype(BF16)
    normed = normed.astype(BF16)
    proj[...] = lax.dot_general(w_ref[...], masked, (((0,), (1,)), ((), ())), preferred_element_type=F32)

    pl.semaphore_wait(barrier, COLS + ROWS - 2)

    def operands(g):
        at = [pl.ds(pl.multiple_of(block * C + g * 8, 8), 8) for block in range(4)]
        left = sigmoid(proj[at[1], :]) * proj[at[0], :]
        right = sigmoid(proj[at[3], :]) * proj[at[2], :]
        return jnp.concatenate([left, right], axis=0).astype(BF16)

    @pl.loop(1, COLS)
    def _(d):
        g = (c + d) % COLS
        send1[g] = operands(g)
        pltpu.make_async_remote_copy(send1.at[g], recv1.at[c], s1.at[d], r1.at[c], (r, g), MESH).start()

    recv1[c] = operands(c)
    gate[...] = sigmoid(jnp.dot(normed, gw_ref[...], preferred_element_type=F32))

    @pl.loop(1, COLS)
    def _(d):
        g = (c + d) % COLS
        pltpu.make_async_copy(recv1.at[g], recv1.at[g], r1.at[g]).wait()

    for b in range(4):
        for a in range(4):
            tiles = [recv1[4 * a + q, :, 128 * b : 128 * b + 128].astype(F32) for q in range(4)]
            for q, tile in enumerate(swap_blocks(tiles)):
                row = 256 * a + 16 * (4 * b + q)
                turn[row : row + 16, :] = tile
    for m in range(16):
        for a in range(4):
            send2[m, :, 128 * a : 128 * a + 128] = turn[pl.ds(256 * a + m, 16, stride=16), :].astype(BF16)

    def put2(n, src, dst, rsem, to):
        pltpu.make_async_remote_copy(src, dst.at[zc], s2.at[n], rsem.at[zc], (to, c), MESH).start()

    @pl.loop(1, NZ)
    def _(d):
        e = (z + d) % NZ
        for k in range(2):
            put2(4 * d + k, send2.at[e], recv_l, r2l, xh * 16 + e * 2 + k)
            put2(4 * d + 2 + k, send2.at[NZ + e], recv_r, r2r, k * 16 + e * 2 + xh)

    put2(0, send2.at[z], recv_l, r2l, r + 1 - 2 * core)
    put2(1, send2.at[NZ + z], recv_r, r2r, (1 - xh) * 16 + z * 2 + xh)
    recv_l[zc] = send2[z]

    @pl.when(core != xh)
    def _():
        put2(2, send2.at[NZ + z], recv_r, r2r, r + 1 - 2 * core)

    @pl.when(core == xh)
    def _():
        recv_r[zc] = send2[NZ + z]

    @pl.loop(0, 16)
    def _(m):
        @pl.when(m != zc)
        def _():
            pltpu.make_async_copy(recv_l.at[m], recv_l.at[m], r2l.at[m]).wait()

        @pl.when(jnp.logical_or(m != zc, core != xh))
        def _():
            pltpu.make_async_copy(recv_r.at[m], recv_r.at[m], r2r.at[m]).wait()

    tri = lax.dot_general(
        recv_l[...].reshape(256, N), recv_r[...].reshape(256, N), (((1,), (1,)), ((), ())), preferred_element_type=F32
    )
    send3[...] = tri.astype(BF16).reshape(16, IL, 256)

    @pl.loop(1, 16)
    def _(d):
        to = (zc + d) % 16
        pltpu.make_async_remote_copy(
            send3.at[to], recv3.at[zc], s3.at[d], r3.at[zc], (xh * 16 + to, c), MESH
        ).start()

    recv3[zc] = send3[zc]

    @pl.loop(1, 16)
    def _(d):
        m = (zc + d) % 16
        pltpu.make_async_copy(recv3.at[m], recv3.at[m], r3.at[m]).wait()

    for a in range(2):
        wide3[256 * a : 256 * a + 256, :] = recv3[:, :, 128 * a : 128 * a + 128].astype(F32).reshape(256, 128)
    for half in range(2):
        for a in range(2):
            for b in range(2):
                parts = []
                for il_half in range(2):
                    tiles = []
                    for q in range(4):
                        il = il_half * 8 + b * 4 + q
                        tiles.append(wide3[pl.ds(256 * a + half * 16 + il, 8, stride=32), :])
                    parts.append(swap_blocks(tiles))
                for q in range(4):
                    send4[half * 8 + a * 4 + q, :, 128 * b : 128 * b + 128] = jnp.concatenate(
                        [parts[0][q], parts[1][q]], axis=0
                    ).astype(BF16)

    @pl.loop(1, COLS)
    def _(d):
        g = (c + d) % COLS
        pltpu.make_async_remote_copy(send4.at[g], recv4.at[c], s4.at[d], r4.at[c], (r, g), MESH).start()

    recv4[c] = send4[c]

    @pl.loop(1, COLS)
    def _(d):
        g = (c + d) % COLS
        pltpu.make_async_copy(recv4.at[g], recv4.at[g], r4.at[g]).wait()

    got = recv4[...].astype(F32)
    for h in range(2):
        tri_t = got[:, 8 * h : 8 * h + 8, :].reshape(C, 256)
        tnorm = layer_norm(tri_t, 0).astype(BF16)
        prod = lax.dot_general(tnorm, ow_ref[...], (((0,), (0,)), ((), ())), preferred_element_type=F32)
        update = gate[256 * h : 256 * h + 256, :] * prod
        out_ref[8 * h : 8 * h + 8] = update.astype(BF16).reshape(8, KL, C)

    @pl.loop(1, COLS)
    def _(d):
        g = (c + d) % COLS
        pltpu.make_async_copy(send1.at[g], send1.at[g], s1.at[d]).wait()
        pltpu.make_async_copy(send4.at[g], send4.at[g], s4.at[d]).wait()
        pltpu.make_async_copy(send3.at[d], send3.at[d], s3.at[d]).wait()

    @pl.loop(4, 32)
    def _(n):
        pltpu.make_async_copy(send2.at[0], send2.at[0], s2.at[n]).wait()

    for n in range(2):
        pltpu.make_async_copy(send2.at[0], send2.at[0], s2.at[n]).wait()

    @pl.when(core != xh)
    def _():
        pltpu.make_async_copy(send2.at[0], send2.at[0], s2.at[2]).wait()


def body(pair, pair_mask, in_weights, gate_weight, out_weight):
    dma = pltpu.SemaphoreType.DMA
    vmem = pltpu.VMEM
    return pl.pallas_call(
        kernel,
        out_shape=jax.ShapeDtypeStruct((IL, KL, C), BF16),
        in_specs=[pl.BlockSpec(memory_space=pl.ANY)] * 5,
        out_specs=pl.BlockSpec(memory_space=vmem),
        scratch_shapes=[
            vmem((IL, KL, C), BF16),
            vmem((IL, KL), jnp.int32),
            vmem((C, 4 * C), BF16),
            vmem((C, C), BF16),
            vmem((C, C), BF16),
            vmem((4 * C, POS), F32),
            vmem((POS, C), F32),
            vmem((COLS, 16, POS), BF16),
            vmem((COLS, 16, POS), BF16),
            vmem((4 * 256, 128), F32),
            vmem((16, IL, N), BF16),
            vmem((16, IL, N), BF16),
            vmem((16, IL, N), BF16),
            vmem((16, IL, 256), BF16),
            vmem((16, IL, 256), BF16),
            vmem((2 * 256, 128), F32),
            vmem((COLS, 16, 256), BF16),
            vmem((COLS, 16, 256), BF16),
            dma((5,)),
            dma((16,)),
            dma((16,)),
            dma((32,)),
            dma((16,)),
            dma((16,)),
            dma((16,)),
            dma((16,)),
            dma((16,)),
            dma((16,)),
        ],
        compiler_params=pltpu.CompilerParams(
            collective_id=0, has_side_effects=True, vmem_limit_bytes=32 * 1024 * 1024
        ),
        cost_estimate=pl.CostEstimate(flops=170_000_000, bytes_accessed=500_000, transcendentals=200_000),
    )(pair, pair_mask, in_weights, gate_weight, out_weight)


def solution(mesh):
    in_specs = (P("row", "col", None), P("row", "col"), P(), P(), P())
    out_specs = P("row", "col", None)
    return jax.shard_map(body, mesh=mesh, in_specs=in_specs, out_specs=out_specs, check_vma=False)
```

```python
import jax
import jax.numpy as jnp
from jax import lax
from jax.experimental import pallas as pl
from jax.experimental.pallas import tpu as pltpu
from jax.sharding import PartitionSpec as P

MESH = pl.DeviceIdType.MESH
F32 = jnp.float32
BF16 = jnp.bfloat16

ROWS, COLS = 32, 16
NZ = 8
IL, KL = 16, 32
N = 512
POS = IL * KL
C = 128


def layer_norm(values, axis):
    mean = jnp.mean(values, axis=axis, keepdims=True)
    centred = values - mean
    var = jnp.mean(centred * centred, axis=axis, keepdims=True)
    return centred * lax.rsqrt(var + 1e-05)


def sigmoid(x):
    return 0.5 * jnp.tanh(0.5 * x) + 0.5


def swap_blocks(v):
    v = list(v)
    lane = lax.broadcasted_iota(jnp.int32, v[0].shape, 1)
    apart, width = len(v) // 2, 64
    while apart:
        low = (lane % (2 * width)) < width
        for n in range(len(v)):
            if n % (2 * apart) < apart:
                x, y = v[n], v[n + apart]
                v[n] = jnp.where(low, x, pltpu.roll(y, width, 1))
                v[n + apart] = jnp.where(low, pltpu.roll(x, 128 - width, 1), y)
        apart, width = apart // 2, width // 2
    return v


def landed(ref, sem):
    pltpu.make_async_copy(ref, ref, sem).wait()


def kernel(
    pair_hbm, mask_hbm, w_hbm, gw_hbm, ow_hbm, out_ref,
    pair_ref, mask_ref, w_ref, gw_ref, ow_ref, proj, gate,
    send_l1, recv_l1, send_r1, recv_r1, turn_l, turn_r, send_l2, recv_l2, send_r2, recv_r2, turn_r2, right,
    tri_ref, send_a3, recv_a3, wide_a, send_a4, recv_a4, send_b3, recv_b3, wide_b, send_b4, recv_b4, ow_wide, ow_turned,
    load_sem, sl1, rl1, sr1, rr1, sl2, rl2, sr2, rr2, s3a, r3a, s4a, r4a, s3b, r3b, s4b, r4b,
):
    r, c = lax.axis_index("row"), lax.axis_index("col")
    xh, z, core = r // 16, (r // 2) % NZ, r % 2
    zc = r % 16

    def far(n):
        return 4 + (1 - 2 * (n % 2)) * ((n + 1) // 2)

    def col_peer(n):
        return (c // 8 + 1 - n % 2) % 2 * 8 + (c + far(n // 2)) % 8

    def zc_peer(n):
        return (z + far(n // 2)) % NZ * 2 + (core + 1 - n % 2) % 2

    def row(xh, z, core):
        return xh * 16 + z * 2 + core

    def send(src, dst, ssem, rsem, to_row, to_col):
        pltpu.make_async_remote_copy(src, dst, ssem, rsem, (to_row, to_col), MESH).start()

    loads = []
    for n, (src, dst) in enumerate(
        ((pair_hbm, pair_ref), (mask_hbm, mask_ref), (w_hbm, w_ref), (gw_hbm, gw_ref), (ow_hbm, ow_ref))
    ):
        loads.append(pltpu.make_async_copy(src, dst, load_sem.at[n]))
        loads[-1].start()

    barrier = pltpu.get_barrier_semaphore()

    def greet(to_row, to_col):
        pl.semaphore_signal(barrier, inc=1, device_id=(to_row, to_col), device_id_type=MESH)

    @pl.loop(1, COLS)
    def _(d):
        greet(r, (c + d) % COLS)

    @pl.loop(0, COLS)
    def _(d):
        greet((r + 16) % ROWS, (c + d) % COLS)

    @pl.loop(1, 16)
    def _(d):
        greet(xh * 16 + (zc + d) % 16, c)

    for load in loads:
        load.wait()

    normed = layer_norm(pair_ref[...].reshape(POS, C).astype(F32), 1)
    eye = lax.broadcasted_iota(jnp.int32, (KL, KL), 0) == lax.broadcasted_iota(jnp.int32, (KL, KL), 1)
    maskf = mask_ref[...].astype(F32)
    column = jnp.concatenate(
        [jnp.sum(jnp.where(eye, maskf[il : il + 1, :], 0.0), axis=1, keepdims=True) for il in range(IL)], axis=0
    )
    masked = (normed * column).astype(BF16)
    normed = normed.astype(BF16)
    full = lax.dot_general(w_ref[...], masked, (((0,), (1,)), ((), ())), preferred_element_type=F32)
    for t in range(4):
        proj[512 * t : 512 * t + 512, :] = full[:, 128 * t : 128 * t + 128]

    pl.semaphore_wait(barrier, 46)

    def left_of(g):
        x = []
        for t in range(4):
            at = [pl.ds(pl.multiple_of(512 * t + block * C + g * 8, 8), 8) for block in range(2)]
            x.append(sigmoid(proj[at[1], :]) * proj[at[0], :])
        x = [jnp.concatenate([x[n], x[n + 2]], axis=0) for n in range(2)]
        return jnp.concatenate(x, axis=1).astype(BF16)

    def right_of(e):
        x = []
        for t in range(4):
            at = [pl.ds(512 * t + block * C + e, 16, stride=8) for block in (2, 3)]
            x.append(sigmoid(proj[at[1], :]) * proj[at[0], :])
        return jnp.concatenate(x, axis=1).astype(BF16)

    def put_left1(n):
        g = col_peer(n)
        send_l1[g] = left_of(g)
        send(send_l1.at[g], recv_l1.at[c], sl1.at[g], rl1.at[c], r, g)

    @pl.loop(0, 7)
    def _(n):
        e = (z + far(n)) % NZ
        send_r1[e] = right_of(e)
        send(send_r1.at[e], recv_r1.at[z], sr1.at[e], rr1.at[z], row(xh, e, core), c)
        put_left1(2 * n)
        put_left1(2 * n + 1)

    put_left1(14)
    recv_r1[z] = right_of(z)
    recv_l1[c] = left_of(c)
    @pl.loop(0, 7)
    def _(n):
        e = (z + far(n)) % NZ
        landed(recv_r1.at[e], rr1.at[e])

    for t in range(4):
        turn_r[128 * t : 128 * t + 128, :] = recv_r1[:, :, 128 * t : 128 * t + 128].astype(F32).reshape(128, 128)
    for g in range(COLS):
        x = [turn_r[pl.ds(128 * t + g, 8, stride=16), :] for t in range(4)]
        for n in range(2):
            send_r2[g, :, 128 * n : 128 * n + 128] = jnp.concatenate([x[n], x[n + 2]], axis=0).astype(BF16)

    @pl.loop(0, 31)
    def _(n):
        g, to = col_peer(n // 2), (xh + 1 - n % 2) % 2
        send(send_r2.at[g], recv_r2.at[xh * 16 + c], sr2.at[n], rr2.at[xh * 16 + c], row(to, z, core), g)

    recv_r2[xh * 16 + c] = send_r2[c]

    @pl.loop(0, 15)
    def _(n):
        g = col_peer(n)
        landed(recv_l1.at[g], rl1.at[g])

    for a in range(4):
        for b in range(2):
            tiles = [recv_l1[4 * a + q, :, 128 * b : 128 * b + 128].astype(F32) for q in range(4)]
            for q, tile in enumerate(swap_blocks(tiles)):
                at = 128 * a + 16 * (4 * b + q)
                turn_l[at : at + 16, :] = tile
    for e in range(NZ):
        for a in range(4):
            x = [turn_l[pl.ds(128 * a + 8 * h + e, 8, stride=16), :] for h in range(2)]
            send_l2[e, :, 128 * a : 128 * a + 128] = jnp.concatenate(x, axis=0).astype(BF16)

    @pl.loop(0, 15)
    def _(n):
        to = zc_peer(n)
        send(send_l2.at[to // 2], recv_l2.at[zc], sl2.at[to], rl2.at[zc], xh * 16 + to, c)

    recv_l2[zc] = send_l2[z]

    ow_wide[...] = ow_ref[...].astype(F32)
    for e in range(NZ):
        ow_turned[16 * e : 16 * e + 16, :] = ow_wide[pl.ds(e, 16, stride=8), :].astype(BF16)
    gate[...] = sigmoid(jnp.dot(normed, gw_ref[...], preferred_element_type=F32)).reshape(IL, KL, C)

    @pl.loop(1, 32)
    def _(d):
        m = (xh * 16 + c + d) % 32
        landed(recv_r2.at[m], rr2.at[m])

    for h in range(2):
        for a in range(4):
            for b in range(2):
                tiles = [recv_r2[16 * h + 4 * a + q, :, 128 * b : 128 * b + 128].astype(F32) for q in range(4)]
                for q, tile in enumerate(swap_blocks(tiles)):
                    at = 256 * a + 128 * h + 16 * (4 * b + q)
                    turn_r2[at : at + 16, :] = tile
        for m in range(NZ):
            for a in range(4):
                x = [turn_r2[pl.ds(256 * a + 128 * h + 8 * jh + m, 8, stride=16), :] for jh in range(2)]
                at = 128 * h + 16 * m
                right[at : at + 16, 128 * a : 128 * a + 128] = jnp.concatenate(x, axis=0).astype(BF16)

    @pl.loop(0, 15)
    def _(n):
        m = zc_peer(n)
        landed(recv_l2.at[m], rl2.at[m])

    tri = lax.dot_general(
        recv_l2[...].reshape(256, N), right[...], (((1,), (1,)), ((), ())), preferred_element_type=F32
    )
    upper = tri.reshape(16, 2, 8, 256)[:, 0]
    send_a3[...] = jnp.concatenate([upper[:, :, :128], upper[:, :, 128:]], axis=1).astype(BF16)

    @pl.loop(0, 15)
    def _(n):
        to = zc_peer(n)
        send(send_a3.at[to], recv_a3.at[zc], s3a.at[to], r3a.at[zc], xh * 16 + to, c)

    for a in range(2):
        tri_ref[256 * a : 256 * a + 256, :] = tri[:, 128 * a : 128 * a + 128]
    for a in range(2):
        tiles = [tri_ref[pl.ds(256 * a + 8 + q, 16, stride=16), :] for q in range(8)]
        for q, tile in enumerate(swap_blocks(tiles)):
            send_b3[8 * a + q] = tile.astype(BF16)

    @pl.loop(0, 15)
    def _(n):
        g = col_peer(n)
        send(send_b3.at[g], recv_b3.at[c], s3b.at[g], r3b.at[c], r, g)

    recv_a3[zc] = send_a3[zc]
    recv_b3[c] = send_b3[c]

    @pl.loop(0, 15)
    def _(n):
        m = zc_peer(n)
        landed(recv_a3.at[m], r3a.at[m])

    wide_a[...] = recv_a3[...].astype(F32).reshape(256, 128)
    for a in range(2):
        parts = []
        for k in range(2):
            parts.append(swap_blocks([wide_a[pl.ds(16 * k + 8 * a + q, 8, stride=32), :] for q in range(8)]))
        for q in range(8):
            send_a4[8 * a + q] = jnp.concatenate([parts[0][q], parts[1][q]], axis=0).astype(BF16)

    @pl.loop(0, 15)
    def _(n):
        g = col_peer(n)
        send(send_a4.at[g], recv_a4.at[c], s4a.at[g], r4a.at[c], r, g)

    @pl.loop(0, 15)
    def _(n):
        g = col_peer(n)
        landed(recv_b3.at[g], r3b.at[g])

    wide_b[...] = recv_b3[...].astype(F32).reshape(256, 128)
    for m in range(16):
        send_b4[m] = wide_b[pl.ds(m, 16, stride=16), :].astype(BF16)

    @pl.loop(0, 15)
    def _(n):
        to = zc_peer(n)
        send(send_b4.at[to], recv_b4.at[zc], s4b.at[to], r4b.at[zc], xh * 16 + to, c)

    recv_a4[c] = send_a4[c]
    recv_b4[zc] = send_b4[zc]

    def finish(tri_t, k, h, weight):
        tnorm = layer_norm(tri_t, 0).astype(BF16)
        prod = lax.dot_general(tnorm, weight, (((0,), (0,)), ((), ())), preferred_element_type=F32)
        update = gate[8 * h : 8 * h + 8, 16 * k : 16 * k + 16, :] * prod.reshape(8, 16, C)
        out_ref[8 * h : 8 * h + 8, 16 * k : 16 * k + 16, :] = update.astype(BF16)

    @pl.loop(0, 15)
    def _(n):
        g = col_peer(n)
        landed(recv_a4.at[g], r4a.at[g])

    got = recv_a4[...].astype(F32)
    for k in range(2):
        finish(got[:, 8 * k : 8 * k + 8, :].reshape(C, 128), k, 0, ow_ref[...])

    @pl.loop(0, 15)
    def _(n):
        m = zc_peer(n)
        landed(recv_b4.at[m], r4b.at[m])

    got = recv_b4[...].astype(F32).reshape(NZ, 2, 16, 128)
    for k in range(2):
        finish(got[:, k].reshape(C, 128), k, 1, ow_turned[...])

    @pl.loop(0, 15)
    def _(n):
        g, m = col_peer(n), zc_peer(n)
        landed(send_l1.at[g], sl1.at[g])
        landed(send_l2.at[0], sl2.at[m])
        landed(send_a3.at[m], s3a.at[m])
        landed(send_b3.at[g], s3b.at[g])
        landed(send_a4.at[g], s4a.at[g])
        landed(send_b4.at[m], s4b.at[m])

    @pl.loop(0, 7)
    def _(n):
        e = (z + far(n)) % NZ
        landed(send_r1.at[e], sr1.at[e])

    @pl.loop(0, 31)
    def _(n):
        landed(send_r2.at[0], sr2.at[n])


def body(pair, pair_mask, in_weights, gate_weight, out_weight):
    dma = pltpu.SemaphoreType.DMA
    vmem = pltpu.VMEM
    return pl.pallas_call(
        kernel,
        out_shape=jax.ShapeDtypeStruct((IL, KL, C), BF16),
        in_specs=[pl.BlockSpec(memory_space=pl.ANY)] * 5,
        out_specs=pl.BlockSpec(memory_space=vmem),
        scratch_shapes=[
            vmem((IL, KL, C), BF16),
            vmem((IL, KL), jnp.int32),
            vmem((C, 4 * C), BF16),
            vmem((C, C), BF16),
            vmem((C, C), BF16),
            vmem((4 * 512, 128), F32),
            vmem((IL, KL, C), F32),
            vmem((COLS, 16, 256), BF16),
            vmem((COLS, 16, 256), BF16),
            vmem((NZ, 16, POS), BF16),
            vmem((NZ, 16, POS), BF16),
            vmem((4 * 128, 128), F32),
            vmem((4 * 128, 128), F32),
            vmem((NZ, 16, N), BF16),
            vmem((16, 16, N), BF16),
            vmem((COLS, 16, 256), BF16),
            vmem((2 * COLS, 16, 256), BF16),
            vmem((4 * 256, 128), F32),
            vmem((256, N), BF16),
            vmem((2 * 256, 128), F32),
            vmem((16, 16, 128), BF16),
            vmem((16, 16, 128), BF16),
            vmem((256, 128), F32),
            vmem((16, 16, 128), BF16),
            vmem((16, 16, 128), BF16),
            vmem((16, 16, 128), BF16),
            vmem((16, 16, 128), BF16),
            vmem((256, 128), F32),
            vmem((16, 16, 128), BF16),
            vmem((16, 16, 128), BF16),
            vmem((C, C), F32),
            vmem((C, C), BF16),
            dma((5,)),
            dma((16,)),
            dma((16,)),
            dma((8,)),
            dma((8,)),
            dma((16,)),
            dma((16,)),
            dma((32,)),
            dma((32,)),
            dma((16,)),
            dma((16,)),
            dma((16,)),
            dma((16,)),
            dma((16,)),
            dma((16,)),
            dma((16,)),
            dma((16,)),
        ],
        compiler_params=pltpu.CompilerParams(
            collective_id=0, has_side_effects=True, vmem_limit_bytes=58 * 1024 * 1024
        ),
        cost_estimate=pl.CostEstimate(flops=170_000_000, bytes_accessed=500_000, transcendentals=200_000),
    )(pair, pair_mask, in_weights, gate_weight, out_weight)


def solution(mesh):
    in_specs = (P("row", "col", None), P("row", "col"), P(), P(), P())
    out_specs = P("row", "col", None)
    return jax.shard_map(body, mesh=mesh, in_specs=in_specs, out_specs=out_specs, check_vma=False)
```

```python
import jax
import jax.numpy as jnp
from jax import lax
from jax.experimental import pallas as pl
from jax.experimental.pallas import tpu as pltpu
from jax.sharding import PartitionSpec as P

MESH = pl.DeviceIdType.MESH
F32 = jnp.float32
BF16 = jnp.bfloat16

ROWS, COLS = 32, 16
NZ = 8
IL, KL = 16, 32
N = 512
POS = IL * KL
C = 128


def layer_norm(values, axis):
    mean = jnp.mean(values, axis=axis, keepdims=True)
    centred = values - mean
    var = jnp.mean(centred * centred, axis=axis, keepdims=True)
    return centred * lax.rsqrt(var + 1e-05)


def sigmoid(x):
    return 0.5 * jnp.tanh(0.5 * x) + 0.5


def swap_blocks(v):
    v = list(v)
    lane = lax.broadcasted_iota(jnp.int32, v[0].shape, 1)
    apart, width = len(v) // 2, 64
    while apart:
        low = (lane % (2 * width)) < width
        for n in range(len(v)):
            if n % (2 * apart) < apart:
                x, y = v[n], v[n + apart]
                v[n] = jnp.where(low, x, pltpu.roll(y, width, 1))
                v[n + apart] = jnp.where(low, pltpu.roll(x, 128 - width, 1), y)
        apart, width = apart // 2, width // 2
    return v


def landed(ref, sem):
    pltpu.make_async_copy(ref, ref, sem).wait()


def kernel(
    pair_hbm, mask_hbm, w_hbm, gw_hbm, ow_hbm, out_ref,
    pair_ref, mask_ref, w_ref, gw_ref, ow_ref, proj, gate,
    send_l1, recv_l1, send_r1, recv_r1, turn_l, turn_r, send_l2, recv_l2, send_r2, recv_r2, turn_r2, right,
    send3, recv3, wide3, send4, recv4,
    met, load_sem, sl1, rl1, sr1, rr1, sl2, rl2, sr2, rr2, s3, r3, s4, r4,
):
    r, c = lax.axis_index("row"), lax.axis_index("col")
    xh, z, core = r // 16, (r // 2) % NZ, r % 2
    zc = r % 16

    def far(n):
        return 4 + (1 - 2 * (n % 2)) * ((n + 1) // 2)

    def col_peer(n):
        return (c // 8 + 1 - n % 2) % 2 * 8 + (c + far(n // 2)) % 8

    def zc_peer(n):
        return (z + far(n // 2)) % NZ * 2 + (core + 1 - n % 2) % 2

    def row(xh, z, core):
        return xh * 16 + z * 2 + core

    def send(src, dst, ssem, rsem, to_row, to_col):
        pltpu.make_async_remote_copy(src, dst, ssem, rsem, (to_row, to_col), MESH).start()

    loads = []
    for n, (src, dst) in enumerate(
        ((pair_hbm, pair_ref), (mask_hbm, mask_ref), (w_hbm, w_ref), (gw_hbm, gw_ref), (ow_hbm, ow_ref))
    ):
        loads.append(pltpu.make_async_copy(src, dst, load_sem.at[n]))
        loads[-1].start()

    barrier = pltpu.get_barrier_semaphore()

    def greet(to_row, to_col):
        pl.semaphore_signal(barrier, inc=1, device_id=(to_row, to_col), device_id_type=MESH)

    sibling, partner = r + 1 - 2 * core, (r + 16) % ROWS

    @pl.loop(1, COLS)
    def _(d):
        greet(r, (c + d) % COLS)

    @pl.loop(1, NZ)
    def _(d):
        greet(row(xh, (z + d) % NZ, core), c)

    greet(sibling, c)
    greet(partner, c)

    for load in loads[:2]:
        load.wait()

    normed = layer_norm(pair_ref[...].reshape(POS, C).astype(F32), 1)
    eye = lax.broadcasted_iota(jnp.int32, (KL, KL), 0) == lax.broadcasted_iota(jnp.int32, (KL, KL), 1)
    maskf = mask_ref[...].astype(F32)
    column = jnp.concatenate(
        [jnp.sum(jnp.where(eye, maskf[il : il + 1, :], 0.0), axis=1, keepdims=True) for il in range(IL)], axis=0
    )
    masked = (normed * column).astype(BF16)
    normed = normed.astype(BF16)
    loads[2].wait()
    full = lax.dot_general(w_ref[...], masked, (((0,), (1,)), ((), ())), preferred_element_type=F32)
    for t in range(4):
        proj[512 * t : 512 * t + 512, :] = full[:, 128 * t : 128 * t + 128]

    pl.semaphore_wait(barrier, 24)
    for to in (sibling, partner):
        pl.semaphore_signal(met, inc=1, device_id=(to, c), device_id_type=MESH)

    def left_of(g):
        x = []
        for t in range(4):
            at = [pl.ds(pl.multiple_of(512 * t + block * C + g * 8, 8), 8) for block in range(2)]
            x.append(sigmoid(proj[at[1], :]) * proj[at[0], :])
        x = [jnp.concatenate([x[n], x[n + 2]], axis=0) for n in range(2)]
        return jnp.concatenate(x, axis=1).astype(BF16)

    def right_of(e):
        x = []
        for t in range(4):
            at = [pl.ds(512 * t + block * C + e, 16, stride=8) for block in (2, 3)]
            x.append(sigmoid(proj[at[1], :]) * proj[at[0], :])
        return jnp.concatenate(x, axis=1).astype(BF16)

    def put_left1(n):
        g = col_peer(n)
        send_l1[g] = left_of(g)
        send(send_l1.at[g], recv_l1.at[c], sl1.at[g], rl1.at[c], r, g)

    @pl.loop(0, 7)
    def _(n):
        e = (z + far(n)) % NZ
        send_r1[e] = right_of(e)
        send(send_r1.at[e], recv_r1.at[z], sr1.at[e], rr1.at[z], row(xh, e, core), c)
        put_left1(2 * n)
        put_left1(2 * n + 1)

    put_left1(14)
    recv_r1[z] = right_of(z)
    recv_l1[c] = left_of(c)
    @pl.loop(0, 7)
    def _(n):
        e = (z + far(n)) % NZ
        landed(recv_r1.at[e], rr1.at[e])

    for t in range(4):
        turn_r[128 * t : 128 * t + 128, :] = recv_r1[:, :, 128 * t : 128 * t + 128].astype(F32).reshape(128, 128)
    for g in range(COLS):
        x = [turn_r[pl.ds(128 * t + g, 8, stride=16), :] for t in range(4)]
        for n in range(2):
            send_r2[g, :, 128 * n : 128 * n + 128] = jnp.concatenate([x[n], x[n + 2]], axis=0).astype(BF16)

    pl.semaphore_wait(met, 2)

    @pl.loop(0, 31)
    def _(n):
        g, to = col_peer(n // 2), (xh + 1 - n % 2) % 2
        send(send_r2.at[g], recv_r2.at[xh * 16 + c], sr2.at[n], rr2.at[xh * 16 + c], row(to, z, core), g)

    recv_r2[xh * 16 + c] = send_r2[c]

    @pl.loop(0, 15)
    def _(n):
        g = col_peer(n)
        landed(recv_l1.at[g], rl1.at[g])

    for a in range(4):
        for b in range(2):
            tiles = [recv_l1[4 * a + q, :, 128 * b : 128 * b + 128].astype(F32) for q in range(4)]
            for q, tile in enumerate(swap_blocks(tiles)):
                at = 128 * a + 16 * (4 * b + q)
                turn_l[at : at + 16, :] = tile
    for e in range(NZ):
        for a in range(4):
            x = [turn_l[pl.ds(128 * a + 8 * h + e, 8, stride=16), :] for h in range(2)]
            send_l2[e, :, 128 * a : 128 * a + 128] = jnp.concatenate(x, axis=0).astype(BF16)

    @pl.loop(0, 7)
    def _(n):
        e = (z + far(n)) % NZ
        send(send_l2.at[e], recv_l2.at[zc], sl2.at[n], rl2.at[zc], row(xh, e, core), c)

    recv_l2[zc] = send_l2[z]
    send(send_l2.at[z], recv_l2.at[zc], sl2.at[7], rl2.at[zc], sibling, c)

    def pass_right(i):
        m = xh * 16 + col_peer(14 - i)
        landed(recv_r2.at[m], rr2.at[m])
        send(recv_r2.at[m], recv_r2.at[m], sr2.at[18 + i], rr2.at[m], partner, c)

    def pass_left(i):
        m = (z + far(6 - i)) % NZ * 2 + core
        landed(recv_l2.at[m], rl2.at[m])
        send(recv_l2.at[m], recv_l2.at[m], sl2.at[8 + i], rl2.at[m], sibling, c)

    @pl.loop(0, 6)
    def _(i):
        pass_left(i)

    pass_left(6)

    loads[3].wait()
    loads[4].wait()
    gate[...] = sigmoid(jnp.dot(normed, gw_ref[...], preferred_element_type=F32)).reshape(IL, KL, C)

    @pl.loop(1, 32)
    def _(d):
        m = (xh * 16 + c + d) % 32
        landed(recv_r2.at[m], rr2.at[m])

    for h in range(2):
        for a in range(4):
            for b in range(2):
                tiles = [recv_r2[16 * h + 4 * a + q, :, 128 * b : 128 * b + 128].astype(F32) for q in range(4)]
                for q, tile in enumerate(swap_blocks(tiles)):
                    at = 256 * a + 128 * h + 16 * (4 * b + q)
                    turn_r2[at : at + 16, :] = tile
        for m in range(NZ):
            for a in range(4):
                x = [turn_r2[pl.ds(256 * a + 128 * h + 8 * jh + m, 8, stride=16), :] for jh in range(2)]
                at = 128 * h + 16 * m
                right[at : at + 16, 128 * a : 128 * a + 128] = jnp.concatenate(x, axis=0).astype(BF16)

    @pl.loop(0, NZ)
    def _(e):
        m = 2 * e + 1 - core
        landed(recv_l2.at[m], rl2.at[m])

    tri = lax.dot_general(
        recv_l2[...].reshape(256, N), right[...], (((1,), (1,)), ((), ())), preferred_element_type=F32
    )
    send3[...] = tri.astype(BF16).reshape(16, IL, 256)

    @pl.loop(0, 15)
    def _(n):
        to = zc_peer(n)
        send(send3.at[to], recv3.at[zc], s3.at[to], r3.at[zc], xh * 16 + to, c)

    recv3[zc] = send3[zc]

    @pl.loop(0, 15)
    def _(n):
        m = zc_peer(n)
        landed(recv3.at[m], r3.at[m])

    for a in range(2):
        wide3[256 * a : 256 * a + 256, :] = recv3[:, :, 128 * a : 128 * a + 128].astype(F32).reshape(256, 128)
    for a in range(2):
        for k in range(2):
            parts = []
            for h in range(2):
                at = 256 * a + 16 * k + 8 * h
                parts.append(swap_blocks([wide3[pl.ds(at + q, 8, stride=32), :] for q in range(8)]))
            for q in range(8):
                send4[8 * a + q, :, 128 * k : 128 * k + 128] = jnp.concatenate(
                    [parts[0][q], parts[1][q]], axis=0
                ).astype(BF16)

    @pl.loop(0, 15)
    def _(n):
        g = col_peer(n)
        send(send4.at[g], recv4.at[c], s4.at[g], r4.at[c], r, g)

    recv4[c] = send4[c]

    @pl.loop(0, 15)
    def _(n):
        g = col_peer(n)
        landed(recv4.at[g], r4.at[g])

    got = recv4[...].astype(F32)
    for h in range(2):
        tnorm = layer_norm(got[:, 8 * h : 8 * h + 8, :].reshape(C, 256), 0).astype(BF16)
        prod = lax.dot_general(tnorm, ow_ref[...], (((0,), (0,)), ((), ())), preferred_element_type=F32)
        for k in range(2):
            part = prod[128 * k : 128 * k + 128, :].reshape(8, 16, C)
            update = gate[8 * h : 8 * h + 8, 16 * k : 16 * k + 16, :] * part
            out_ref[8 * h : 8 * h + 8, 16 * k : 16 * k + 16, :] = update.astype(BF16)

    @pl.loop(0, 15)
    def _(n):
        g, m = col_peer(n), zc_peer(n)
        landed(send_l1.at[g], sl1.at[g])
        landed(send_l2.at[0], sl2.at[n])
        landed(send3.at[m], s3.at[m])
        landed(send4.at[g], s4.at[g])

    @pl.loop(0, 7)
    def _(n):
        e = (z + far(n)) % NZ
        landed(send_r1.at[e], sr1.at[e])

    @pl.loop(0, 31)
    def _(n):
        landed(send_r2.at[0], sr2.at[n])


def body(pair, pair_mask, in_weights, gate_weight, out_weight):
    dma = pltpu.SemaphoreType.DMA
    vmem = pltpu.VMEM
    return pl.pallas_call(
        kernel,
        out_shape=jax.ShapeDtypeStruct((IL, KL, C), BF16),
        in_specs=[pl.BlockSpec(memory_space=pl.ANY)] * 5,
        out_specs=pl.BlockSpec(memory_space=vmem),
        scratch_shapes=[
            vmem((IL, KL, C), BF16),
            vmem((IL, KL), jnp.int32),
            vmem((C, 4 * C), BF16),
            vmem((C, C), BF16),
            vmem((C, C), BF16),
            vmem((4 * 512, 128), F32),
            vmem((IL, KL, C), F32),
            vmem((COLS, 16, 256), BF16),
            vmem((COLS, 16, 256), BF16),
            vmem((NZ, 16, POS), BF16),
            vmem((NZ, 16, POS), BF16),
            vmem((4 * 128, 128), F32),
            vmem((4 * 128, 128), F32),
            vmem((NZ, 16, N), BF16),
            vmem((16, 16, N), BF16),
            vmem((COLS, 16, 256), BF16),
            vmem((2 * COLS, 16, 256), BF16),
            vmem((4 * 256, 128), F32),
            vmem((256, N), BF16),
            vmem((16, IL, 256), BF16),
            vmem((16, IL, 256), BF16),
            vmem((2 * 256, 128), F32),
            vmem((COLS, 16, 256), BF16),
            vmem((COLS, 16, 256), BF16),
            pltpu.SemaphoreType.REGULAR,
            dma((5,)),
            dma((16,)),
            dma((16,)),
            dma((8,)),
            dma((8,)),
            dma((16,)),
            dma((16,)),
            dma((32,)),
            dma((32,)),
            dma((16,)),
            dma((16,)),
            dma((16,)),
            dma((16,)),
        ],
        compiler_params=pltpu.CompilerParams(
            collective_id=0, has_side_effects=True, vmem_limit_bytes=58 * 1024 * 1024
        ),
        cost_estimate=pl.CostEstimate(flops=170_000_000, bytes_accessed=500_000, transcendentals=200_000),
    )(pair, pair_mask, in_weights, gate_weight, out_weight)


def solution(mesh):
    in_specs = (P("row", "col", None), P("row", "col"), P(), P(), P())
    out_specs = P("row", "col", None)
    return jax.shard_map(body, mesh=mesh, in_specs=in_specs, out_specs=out_specs, check_vma=False)
```

```python
import jax
import jax.numpy as jnp
from jax import lax
from jax.experimental import pallas as pl
from jax.experimental.pallas import tpu as pltpu
from jax.sharding import PartitionSpec as P

MESH = pl.DeviceIdType.MESH
F32 = jnp.float32
BF16 = jnp.bfloat16

ROWS, COLS = 32, 16
NZ = 8
IL, KL = 16, 32
N = 512
POS = IL * KL
C = 128


def layer_norm(values, axis):
    mean = jnp.mean(values, axis=axis, keepdims=True)
    centred = values - mean
    var = jnp.mean(centred * centred, axis=axis, keepdims=True)
    return centred * lax.rsqrt(var + 1e-05)


def sigmoid(x):
    return 0.5 * jnp.tanh(0.5 * x) + 0.5


def swap_blocks(v):
    v = list(v)
    lane = lax.broadcasted_iota(jnp.int32, v[0].shape, 1)
    apart, width = len(v) // 2, 64
    while apart:
        low = (lane % (2 * width)) < width
        for n in range(len(v)):
            if n % (2 * apart) < apart:
                x, y = v[n], v[n + apart]
                v[n] = jnp.where(low, x, pltpu.roll(y, width, 1))
                v[n + apart] = jnp.where(low, pltpu.roll(x, 128 - width, 1), y)
        apart, width = apart // 2, width // 2
    return v


def landed(ref, sem):
    pltpu.make_async_copy(ref, ref, sem).wait()


def kernel(
    pair_hbm, mask_hbm, w_hbm, gw_hbm, ow_hbm, out_ref,
    pair_ref, mask_ref, w_ref, gw_ref, ow_ref, proj, gate,
    send_l1, recv_l1, send_r1, recv_r1, turn_l, turn_r, send_l2, recv_l2, send_r2, recv_r2, turn_r2, right,
    send3, recv3, wide3, send4, recv4,
    met, load_sem, sl1, rl1, sr1, rr1, sl2, rl2, sr2, rr2, s3, r3, s4, r4,
):
    r, c = lax.axis_index("row"), lax.axis_index("col")
    xh, z, core = r // 16, (r // 2) % NZ, r % 2
    zc = r % 16

    def far(n):
        return 4 + (1 - 2 * (n % 2)) * ((n + 1) // 2)

    def col_peer(n):
        return (c // 8 + 1 - n % 2) % 2 * 8 + (c + far(n // 2)) % 8

    def zc_peer(n):
        return (z + far(n // 2)) % NZ * 2 + (core + 1 - n % 2) % 2

    def row(xh, z, core):
        return xh * 16 + z * 2 + core

    def send(src, dst, ssem, rsem, to_row, to_col):
        pltpu.make_async_remote_copy(src, dst, ssem, rsem, (to_row, to_col), MESH).start()

    loads = []
    for n, (src, dst) in enumerate(
        ((pair_hbm, pair_ref), (mask_hbm, mask_ref), (w_hbm, w_ref), (gw_hbm, gw_ref), (ow_hbm, ow_ref))
    ):
        loads.append(pltpu.make_async_copy(src, dst, load_sem.at[n]))
        loads[-1].start()

    barrier = pltpu.get_barrier_semaphore()

    def greet(to_row, to_col):
        pl.semaphore_signal(barrier, inc=1, device_id=(to_row, to_col), device_id_type=MESH)

    sibling, partner = r + 1 - 2 * core, (r + 16) % ROWS

    @pl.loop(1, COLS)
    def _(d):
        greet(r, (c + d) % COLS)

    @pl.loop(1, NZ)
    def _(d):
        greet(row(xh, (z + d) % NZ, core), c)

    greet(sibling, c)
    greet(partner, c)

    for load in loads[:2]:
        load.wait()

    normed = layer_norm(pair_ref[...].reshape(POS, C).astype(F32), 1)
    eye = lax.broadcasted_iota(jnp.int32, (KL, KL), 0) == lax.broadcasted_iota(jnp.int32, (KL, KL), 1)
    maskf = mask_ref[...].astype(F32)
    column = jnp.concatenate(
        [jnp.sum(jnp.where(eye, maskf[il : il + 1, :], 0.0), axis=1, keepdims=True) for il in range(IL)], axis=0
    )
    masked = (normed * column).astype(BF16)
    normed = normed.astype(BF16)
    loads[2].wait()
    full = lax.dot_general(w_ref[...], masked, (((0,), (1,)), ((), ())), preferred_element_type=F32)
    for t in range(4):
        proj[512 * t : 512 * t + 512, :] = full[:, 128 * t : 128 * t + 128]

    pl.semaphore_wait(barrier, 24)
    for to in (sibling, partner):
        pl.semaphore_signal(met, inc=1, device_id=(to, c), device_id_type=MESH)

    def left_of(g):
        x = []
        for t in range(4):
            at = [pl.ds(pl.multiple_of(512 * t + block * C + g * 8, 8), 8) for block in range(2)]
            x.append(sigmoid(proj[at[1], :]) * proj[at[0], :])
        x = [jnp.concatenate([x[n], x[n + 2]], axis=0) for n in range(2)]
        return jnp.concatenate(x, axis=1).astype(BF16)

    def right_of(e):
        x = []
        for t in range(4):
            at = [pl.ds(512 * t + block * C + e, 16, stride=8) for block in (2, 3)]
            x.append(sigmoid(proj[at[1], :]) * proj[at[0], :])
        return jnp.concatenate(x, axis=1).astype(BF16)

    def put_left1(n):
        g = col_peer(n)
        send_l1[g] = left_of(g)
        send(send_l1.at[g], recv_l1.at[c], sl1.at[g], rl1.at[c], r, g)

    @pl.loop(0, 7)
    def _(n):
        e = (z + far(n)) % NZ
        send_r1[e] = right_of(e)
        send(send_r1.at[e], recv_r1.at[z], sr1.at[e], rr1.at[z], row(xh, e, core), c)
        put_left1(2 * n)
        put_left1(2 * n + 1)

    put_left1(14)
    recv_r1[z] = right_of(z)
    recv_l1[c] = left_of(c)
    @pl.loop(0, 7)
    def _(n):
        e = (z + far(n)) % NZ
        landed(recv_r1.at[e], rr1.at[e])

    for t in range(4):
        turn_r[128 * t : 128 * t + 128, :] = recv_r1[:, :, 128 * t : 128 * t + 128].astype(F32).reshape(128, 128)
    for g in range(COLS):
        x = [turn_r[pl.ds(128 * t + g, 8, stride=16), :] for t in range(4)]
        for n in range(2):
            send_r2[g, :, 128 * n : 128 * n + 128] = jnp.concatenate([x[n], x[n + 2]], axis=0).astype(BF16)

    pl.semaphore_wait(met, 2)

    @pl.loop(0, 31)
    def _(n):
        g, to = col_peer(n % 16), (xh + 1 - n // 16) % 2
        send(send_r2.at[g], recv_r2.at[xh * 16 + c], sr2.at[n], rr2.at[xh * 16 + c], row(to, z, core), g)

    recv_r2[xh * 16 + c] = send_r2[c]

    @pl.loop(0, 15)
    def _(n):
        g = col_peer(n)
        landed(recv_l1.at[g], rl1.at[g])

    for a in range(4):
        for b in range(2):
            tiles = [recv_l1[4 * a + q, :, 128 * b : 128 * b + 128].astype(F32) for q in range(4)]
            for q, tile in enumerate(swap_blocks(tiles)):
                at = 128 * a + 16 * (4 * b + q)
                turn_l[at : at + 16, :] = tile
    for e in range(NZ):
        for a in range(4):
            x = [turn_l[pl.ds(128 * a + 8 * h + e, 8, stride=16), :] for h in range(2)]
            send_l2[e, :, 128 * a : 128 * a + 128] = jnp.concatenate(x, axis=0).astype(BF16)

    @pl.loop(0, 7)
    def _(n):
        e = (z + far(n)) % NZ
        send(send_l2.at[e], recv_l2.at[zc], sl2.at[n], rl2.at[zc], row(xh, e, core), c)

    recv_l2[zc] = send_l2[z]
    send(send_l2.at[z], recv_l2.at[zc], sl2.at[7], rl2.at[zc], sibling, c)

    def pass_right(i):
        m = xh * 16 + col_peer(14 - i)
        landed(recv_r2.at[m], rr2.at[m])
        send(recv_r2.at[m], recv_r2.at[m], sr2.at[18 + i], rr2.at[m], partner, c)

    def pass_left(i):
        m = (z + far(6 - i)) % NZ * 2 + core
        landed(recv_l2.at[m], rl2.at[m])
        send(recv_l2.at[m], recv_l2.at[m], sl2.at[8 + i], rl2.at[m], sibling, c)

    @pl.loop(0, 6)
    def _(i):
        pass_left(i)

    pass_left(6)

    loads[3].wait()
    loads[4].wait()
    gate[...] = sigmoid(jnp.dot(normed, gw_ref[...], preferred_element_type=F32)).reshape(IL, KL, C)

    @pl.loop(1, 32)
    def _(d):
        m = (xh * 16 + c + d) % 32
        landed(recv_r2.at[m], rr2.at[m])

    for h in range(2):
        for a in range(4):
            for b in range(2):
                tiles = [recv_r2[16 * h + 4 * a + q, :, 128 * b : 128 * b + 128].astype(F32) for q in range(4)]
                for q, tile in enumerate(swap_blocks(tiles)):
                    at = 256 * a + 128 * h + 16 * (4 * b + q)
                    turn_r2[at : at + 16, :] = tile
        for m in range(NZ):
            for a in range(4):
                x = [turn_r2[pl.ds(256 * a + 128 * h + 8 * jh + m, 8, stride=16), :] for jh in range(2)]
                at = 128 * h + 16 * m
                right[at : at + 16, 128 * a : 128 * a + 128] = jnp.concatenate(x, axis=0).astype(BF16)

    @pl.loop(0, NZ)
    def _(e):
        m = 2 * e + 1 - core
        landed(recv_l2.at[m], rl2.at[m])

    tri = lax.dot_general(
        recv_l2[...].reshape(256, N), right[...], (((1,), (1,)), ((), ())), preferred_element_type=F32
    )
    send3[...] = tri.astype(BF16).reshape(16, IL, 256)

    @pl.loop(0, 15)
    def _(n):
        to = zc_peer(n)
        send(send3.at[to], recv3.at[zc], s3.at[to], r3.at[zc], xh * 16 + to, c)

    recv3[zc] = send3[zc]

    @pl.loop(0, 15)
    def _(n):
        m = zc_peer(n)
        landed(recv3.at[m], r3.at[m])

    for a in range(2):
        wide3[256 * a : 256 * a + 256, :] = recv3[:, :, 128 * a : 128 * a + 128].astype(F32).reshape(256, 128)
    for a in range(2):
        for k in range(2):
            parts = []
            for h in range(2):
                at = 256 * a + 16 * k + 8 * h
                parts.append(swap_blocks([wide3[pl.ds(at + q, 8, stride=32), :] for q in range(8)]))
            for q in range(8):
                send4[8 * a + q, :, 128 * k : 128 * k + 128] = jnp.concatenate(
                    [parts[0][q], parts[1][q]], axis=0
                ).astype(BF16)

    @pl.loop(0, 15)
    def _(n):
        g = col_peer(n)
        send(send4.at[g], recv4.at[c], s4.at[g], r4.at[c], r, g)

    recv4[c] = send4[c]

    @pl.loop(0, 15)
    def _(n):
        g = col_peer(n)
        landed(recv4.at[g], r4.at[g])

    got = recv4[...].astype(F32)
    for h in range(2):
        tnorm = layer_norm(got[:, 8 * h : 8 * h + 8, :].reshape(C, 256), 0).astype(BF16)
        prod = lax.dot_general(tnorm, ow_ref[...], (((0,), (0,)), ((), ())), preferred_element_type=F32)
        for k in range(2):
            part = prod[128 * k : 128 * k + 128, :].reshape(8, 16, C)
            update = gate[8 * h : 8 * h + 8, 16 * k : 16 * k + 16, :] * part
            out_ref[8 * h : 8 * h + 8, 16 * k : 16 * k + 16, :] = update.astype(BF16)

    @pl.loop(0, 15)
    def _(n):
        g, m = col_peer(n), zc_peer(n)
        landed(send_l1.at[g], sl1.at[g])
        landed(send_l2.at[0], sl2.at[n])
        landed(send3.at[m], s3.at[m])
        landed(send4.at[g], s4.at[g])

    @pl.loop(0, 7)
    def _(n):
        e = (z + far(n)) % NZ
        landed(send_r1.at[e], sr1.at[e])

    @pl.loop(0, 31)
    def _(n):
        landed(send_r2.at[0], sr2.at[n])


def body(pair, pair_mask, in_weights, gate_weight, out_weight):
    dma = pltpu.SemaphoreType.DMA
    vmem = pltpu.VMEM
    return pl.pallas_call(
        kernel,
        out_shape=jax.ShapeDtypeStruct((IL, KL, C), BF16),
        in_specs=[pl.BlockSpec(memory_space=pl.ANY)] * 5,
        out_specs=pl.BlockSpec(memory_space=vmem),
        scratch_shapes=[
            vmem((IL, KL, C), BF16),
            vmem((IL, KL), jnp.int32),
            vmem((C, 4 * C), BF16),
            vmem((C, C), BF16),
            vmem((C, C), BF16),
            vmem((4 * 512, 128), F32),
            vmem((IL, KL, C), F32),
            vmem((COLS, 16, 256), BF16),
            vmem((COLS, 16, 256), BF16),
            vmem((NZ, 16, POS), BF16),
            vmem((NZ, 16, POS), BF16),
            vmem((4 * 128, 128), F32),
            vmem((4 * 128, 128), F32),
            vmem((NZ, 16, N), BF16),
            vmem((16, 16, N), BF16),
            vmem((COLS, 16, 256), BF16),
            vmem((2 * COLS, 16, 256), BF16),
            vmem((4 * 256, 128), F32),
            vmem((256, N), BF16),
            vmem((16, IL, 256), BF16),
            vmem((16, IL, 256), BF16),
            vmem((2 * 256, 128), F32),
            vmem((COLS, 16, 256), BF16),
            vmem((COLS, 16, 256), BF16),
            pltpu.SemaphoreType.REGULAR,
            dma((5,)),
            dma((16,)),
            dma((16,)),
            dma((8,)),
            dma((8,)),
            dma((16,)),
            dma((16,)),
            dma((32,)),
            dma((32,)),
            dma((16,)),
            dma((16,)),
            dma((16,)),
            dma((16,)),
        ],
        compiler_params=pltpu.CompilerParams(
            collective_id=0, has_side_effects=True, vmem_limit_bytes=58 * 1024 * 1024
        ),
        cost_estimate=pl.CostEstimate(flops=170_000_000, bytes_accessed=500_000, transcendentals=200_000),
    )(pair, pair_mask, in_weights, gate_weight, out_weight)


def solution(mesh):
    in_specs = (P("row", "col", None), P("row", "col"), P(), P(), P())
    out_specs = P("row", "col", None)
    return jax.shard_map(body, mesh=mesh, in_specs=in_specs, out_specs=out_specs, check_vma=False)
```

```python
import jax
import jax.numpy as jnp
from jax import lax
from jax.experimental import pallas as pl
from jax.experimental.pallas import tpu as pltpu
from jax.sharding import PartitionSpec as P

MESH = pl.DeviceIdType.MESH
F32 = jnp.float32
BF16 = jnp.bfloat16

ROWS, COLS = 32, 16
NZ = 8
IL, KL = 16, 32
N = 512
POS = IL * KL
C = 128


def layer_norm(values, axis):
    mean = jnp.mean(values, axis=axis, keepdims=True)
    centred = values - mean
    var = jnp.mean(centred * centred, axis=axis, keepdims=True)
    return centred * lax.rsqrt(var + 1e-05)


def sigmoid(x):
    return 0.5 * jnp.tanh(0.5 * x) + 0.5


def swap_blocks(v):
    v = list(v)
    lane = lax.broadcasted_iota(jnp.int32, v[0].shape, 1)
    apart, width = len(v) // 2, 64
    while apart:
        low = (lane % (2 * width)) < width
        for n in range(len(v)):
            if n % (2 * apart) < apart:
                x, y = v[n], v[n + apart]
                v[n] = jnp.where(low, x, pltpu.roll(y, width, 1))
                v[n + apart] = jnp.where(low, pltpu.roll(x, 128 - width, 1), y)
        apart, width = apart // 2, width // 2
    return v


def landed(ref, sem):
    pltpu.make_async_copy(ref, ref, sem).wait()


def kernel(
    pair_hbm, mask_hbm, w_hbm, gw_hbm, ow_hbm, out_ref,
    pair_ref, mask_ref, w_ref, gw_ref, ow_ref, proj, gate,
    send_l1, recv_l1, send_r1, recv_r1, turn_l, turn_r, send_l2, recv_l2, send_r2, recv_r2, turn_r2, right,
    send3, recv3, wide3, send4, recv4,
    met, load_sem, sl1, rl1, sr1, rr1, sl2, rl2, sr2, rr2, s3, r3, s4, r4,
):
    r, c = lax.axis_index("row"), lax.axis_index("col")
    xh, z, core = r // 16, (r // 2) % NZ, r % 2
    zc = r % 16

    def far(n):
        return 4 + (1 - 2 * (n % 2)) * ((n + 1) // 2)

    def col_peer(n):
        return (c // 8 + 1 - n % 2) % 2 * 8 + (c + far(n // 2)) % 8

    def zc_peer(n):
        return (z + far(n // 2)) % NZ * 2 + (core + 1 - n % 2) % 2

    def row(xh, z, core):
        return xh * 16 + z * 2 + core

    def send(src, dst, ssem, rsem, to_row, to_col):
        pltpu.make_async_remote_copy(src, dst, ssem, rsem, (to_row, to_col), MESH).start()

    loads = []
    for n, (src, dst) in enumerate(
        ((pair_hbm, pair_ref), (mask_hbm, mask_ref), (w_hbm, w_ref), (gw_hbm, gw_ref), (ow_hbm, ow_ref))
    ):
        loads.append(pltpu.make_async_copy(src, dst, load_sem.at[n]))
        loads[-1].start()

    barrier = pltpu.get_barrier_semaphore()

    def greet(to_row, to_col):
        pl.semaphore_signal(barrier, inc=1, device_id=(to_row, to_col), device_id_type=MESH)

    sibling, partner = r + 1 - 2 * core, (r + 16) % ROWS

    @pl.loop(1, COLS)
    def _(d):
        greet(r, (c + d) % COLS)

    @pl.loop(1, NZ)
    def _(d):
        greet(row(xh, (z + d) % NZ, core), c)

    greet(sibling, c)
    greet(partner, c)

    for load in loads[:2]:
        load.wait()

    normed = layer_norm(pair_ref[...].reshape(POS, C).astype(F32), 1)
    eye = lax.broadcasted_iota(jnp.int32, (KL, KL), 0) == lax.broadcasted_iota(jnp.int32, (KL, KL), 1)
    maskf = mask_ref[...].astype(F32)
    column = jnp.concatenate(
        [jnp.sum(jnp.where(eye, maskf[il : il + 1, :], 0.0), axis=1, keepdims=True) for il in range(IL)], axis=0
    )
    masked = (normed * column).astype(BF16)
    normed = normed.astype(BF16)
    loads[2].wait()
    full = lax.dot_general(w_ref[...], masked, (((0,), (1,)), ((), ())), preferred_element_type=F32)
    for t in range(4):
        proj[512 * t : 512 * t + 512, :] = full[:, 128 * t : 128 * t + 128]

    pl.semaphore_wait(barrier, 24)
    for to in (sibling, partner):
        pl.semaphore_signal(met, inc=1, device_id=(to, c), device_id_type=MESH)

    def left_of(g):
        x = []
        for t in range(4):
            at = [pl.ds(pl.multiple_of(512 * t + block * C + g * 8, 8), 8) for block in range(2)]
            x.append(sigmoid(proj[at[1], :]) * proj[at[0], :])
        x = [jnp.concatenate([x[n], x[n + 2]], axis=0) for n in range(2)]
        return jnp.concatenate(x, axis=1).astype(BF16)

    def right_of(e):
        x = []
        for t in range(4):
            at = [pl.ds(512 * t + block * C + e, 16, stride=8) for block in (2, 3)]
            x.append(sigmoid(proj[at[1], :]) * proj[at[0], :])
        return jnp.concatenate(x, axis=1).astype(BF16)

    def put_left1(n):
        g = col_peer(n)
        send_l1[g] = left_of(g)
        send(send_l1.at[g], recv_l1.at[c], sl1.at[g], rl1.at[c], r, g)

    @pl.loop(0, 7)
    def _(n):
        e = (z + far(n)) % NZ
        send_r1[e] = right_of(e)
        send(send_r1.at[e], recv_r1.at[z], sr1.at[e], rr1.at[z], row(xh, e, core), c)
        put_left1(2 * n)
        put_left1(2 * n + 1)

    put_left1(14)
    recv_r1[z] = right_of(z)
    recv_l1[c] = left_of(c)
    @pl.loop(0, 7)
    def _(n):
        e = (z + far(n)) % NZ
        landed(recv_r1.at[e], rr1.at[e])

    for t in range(4):
        turn_r[128 * t : 128 * t + 128, :] = recv_r1[:, :, 128 * t : 128 * t + 128].astype(F32).reshape(128, 128)
    for g in range(COLS):
        x = [turn_r[pl.ds(128 * t + g, 8, stride=16), :] for t in range(4)]
        for n in range(2):
            send_r2[g, :, 128 * n : 128 * n + 128] = jnp.concatenate([x[n], x[n + 2]], axis=0).astype(BF16)

    pl.semaphore_wait(met, 2)

    @pl.loop(0, 16)
    def _(n):
        g = col_peer(n + 1 - 2 * (n % 2))
        send(send_r2.at[g], recv_r2.at[xh * 16 + c], sr2.at[n], rr2.at[xh * 16 + c], partner, g)

    @pl.loop(0, 15)
    def _(n):
        g = col_peer(n)
        send(send_r2.at[g], recv_r2.at[xh * 16 + c], sr2.at[16 + n], rr2.at[xh * 16 + c], r, g)

    recv_r2[xh * 16 + c] = send_r2[c]

    @pl.loop(0, 15)
    def _(n):
        g = col_peer(n)
        landed(recv_l1.at[g], rl1.at[g])

    for a in range(4):
        for b in range(2):
            tiles = [recv_l1[4 * a + q, :, 128 * b : 128 * b + 128].astype(F32) for q in range(4)]
            for q, tile in enumerate(swap_blocks(tiles)):
                at = 128 * a + 16 * (4 * b + q)
                turn_l[at : at + 16, :] = tile
    for e in range(NZ):
        for a in range(4):
            x = [turn_l[pl.ds(128 * a + 8 * h + e, 8, stride=16), :] for h in range(2)]
            send_l2[e, :, 128 * a : 128 * a + 128] = jnp.concatenate(x, axis=0).astype(BF16)

    @pl.loop(0, 7)
    def _(n):
        e = (z + far(n)) % NZ
        send(send_l2.at[e], recv_l2.at[zc], sl2.at[n], rl2.at[zc], row(xh, e, core), c)

    recv_l2[zc] = send_l2[z]
    send(send_l2.at[z], recv_l2.at[zc], sl2.at[7], rl2.at[zc], sibling, c)

    def pass_right(i):
        m = xh * 16 + col_peer(14 - i)
        landed(recv_r2.at[m], rr2.at[m])
        send(recv_r2.at[m], recv_r2.at[m], sr2.at[18 + i], rr2.at[m], partner, c)

    def pass_left(i):
        m = (z + far(6 - i)) % NZ * 2 + core
        landed(recv_l2.at[m], rl2.at[m])
        send(recv_l2.at[m], recv_l2.at[m], sl2.at[8 + i], rl2.at[m], sibling, c)

    @pl.loop(0, 6)
    def _(i):
        pass_left(i)

    pass_left(6)

    loads[3].wait()
    loads[4].wait()
    gate[...] = sigmoid(jnp.dot(normed, gw_ref[...], preferred_element_type=F32)).reshape(IL, KL, C)

    for h in range(2):

        @pl.loop(16 * h, 16 * h + 16)
        def _(m):
            @pl.when(m != xh * 16 + c)
            def _():
                landed(recv_r2.at[m], rr2.at[m])

        for a in range(4):
            for b in range(2):
                tiles = [recv_r2[16 * h + 4 * a + q, :, 128 * b : 128 * b + 128].astype(F32) for q in range(4)]
                for q, tile in enumerate(swap_blocks(tiles)):
                    at = 256 * a + 128 * h + 16 * (4 * b + q)
                    turn_r2[at : at + 16, :] = tile
        for m in range(NZ):
            for a in range(4):
                x = [turn_r2[pl.ds(256 * a + 128 * h + 8 * jh + m, 8, stride=16), :] for jh in range(2)]
                at = 128 * h + 16 * m
                right[at : at + 16, 128 * a : 128 * a + 128] = jnp.concatenate(x, axis=0).astype(BF16)

    @pl.loop(0, NZ)
    def _(e):
        m = 2 * e + 1 - core
        landed(recv_l2.at[m], rl2.at[m])

    tri = lax.dot_general(
        recv_l2[...].reshape(256, N), right[...], (((1,), (1,)), ((), ())), preferred_element_type=F32
    )
    send3[...] = tri.astype(BF16).reshape(16, IL, 256)

    @pl.loop(0, 15)
    def _(n):
        to = zc_peer(n)
        send(send3.at[to], recv3.at[zc], s3.at[to], r3.at[zc], xh * 16 + to, c)

    recv3[zc] = send3[zc]

    @pl.loop(0, 15)
    def _(n):
        m = zc_peer(n)
        landed(recv3.at[m], r3.at[m])

    for a in range(2):
        wide3[256 * a : 256 * a + 256, :] = recv3[:, :, 128 * a : 128 * a + 128].astype(F32).reshape(256, 128)
    for a in range(2):
        for k in range(2):
            parts = []
            for h in range(2):
                at = 256 * a + 16 * k + 8 * h
                parts.append(swap_blocks([wide3[pl.ds(at + q, 8, stride=32), :] for q in range(8)]))
            for q in range(8):
                send4[8 * a + q, :, 128 * k : 128 * k + 128] = jnp.concatenate(
                    [parts[0][q], parts[1][q]], axis=0
                ).astype(BF16)

    @pl.loop(0, 15)
    def _(n):
        g = col_peer(n)
        send(send4.at[g], recv4.at[c], s4.at[g], r4.at[c], r, g)

    recv4[c] = send4[c]

    @pl.loop(0, 15)
    def _(n):
        g = col_peer(n)
        landed(recv4.at[g], r4.at[g])

    got = recv4[...].astype(F32)
    for h in range(2):
        tnorm = layer_norm(got[:, 8 * h : 8 * h + 8, :].reshape(C, 256), 0).astype(BF16)
        prod = lax.dot_general(tnorm, ow_ref[...], (((0,), (0,)), ((), ())), preferred_element_type=F32)
        for k in range(2):
            part = prod[128 * k : 128 * k + 128, :].reshape(8, 16, C)
            update = gate[8 * h : 8 * h + 8, 16 * k : 16 * k + 16, :] * part
            out_ref[8 * h : 8 * h + 8, 16 * k : 16 * k + 16, :] = update.astype(BF16)

    @pl.loop(0, 15)
    def _(n):
        g, m = col_peer(n), zc_peer(n)
        landed(send_l1.at[g], sl1.at[g])
        landed(send_l2.at[0], sl2.at[n])
        landed(send3.at[m], s3.at[m])
        landed(send4.at[g], s4.at[g])

    @pl.loop(0, 7)
    def _(n):
        e = (z + far(n)) % NZ
        landed(send_r1.at[e], sr1.at[e])

    @pl.loop(0, 31)
    def _(n):
        landed(send_r2.at[0], sr2.at[n])


def body(pair, pair_mask, in_weights, gate_weight, out_weight):
    dma = pltpu.SemaphoreType.DMA
    vmem = pltpu.VMEM
    return pl.pallas_call(
        kernel,
        out_shape=jax.ShapeDtypeStruct((IL, KL, C), BF16),
        in_specs=[pl.BlockSpec(memory_space=pl.ANY)] * 5,
        out_specs=pl.BlockSpec(memory_space=vmem),
        scratch_shapes=[
            vmem((IL, KL, C), BF16),
            vmem((IL, KL), jnp.int32),
            vmem((C, 4 * C), BF16),
            vmem((C, C), BF16),
            vmem((C, C), BF16),
            vmem((4 * 512, 128), F32),
            vmem((IL, KL, C), F32),
            vmem((COLS, 16, 256), BF16),
            vmem((COLS, 16, 256), BF16),
            vmem((NZ, 16, POS), BF16),
            vmem((NZ, 16, POS), BF16),
            vmem((4 * 128, 128), F32),
            vmem((4 * 128, 128), F32),
            vmem((NZ, 16, N), BF16),
            vmem((16, 16, N), BF16),
            vmem((COLS, 16, 256), BF16),
            vmem((2 * COLS, 16, 256), BF16),
            vmem((4 * 256, 128), F32),
            vmem((256, N), BF16),
            vmem((16, IL, 256), BF16),
            vmem((16, IL, 256), BF16),
            vmem((2 * 256, 128), F32),
            vmem((COLS, 16, 256), BF16),
            vmem((COLS, 16, 256), BF16),
            pltpu.SemaphoreType.REGULAR,
            dma((5,)),
            dma((16,)),
            dma((16,)),
            dma((8,)),
            dma((8,)),
            dma((16,)),
            dma((16,)),
            dma((32,)),
            dma((32,)),
            dma((16,)),
            dma((16,)),
            dma((16,)),
            dma((16,)),
        ],
        compiler_params=pltpu.CompilerParams(
            collective_id=0, has_side_effects=True, vmem_limit_bytes=58 * 1024 * 1024
        ),
        cost_estimate=pl.CostEstimate(flops=170_000_000, bytes_accessed=500_000, transcendentals=200_000),
    )(pair, pair_mask, in_weights, gate_weight, out_weight)


def solution(mesh):
    in_specs = (P("row", "col", None), P("row", "col"), P(), P(), P())
    out_specs = P("row", "col", None)
    return jax.shard_map(body, mesh=mesh, in_specs=in_specs, out_specs=out_specs, check_vma=False)
```

```python
import jax
import jax.numpy as jnp
from jax import lax
from jax.experimental import pallas as pl
from jax.experimental.pallas import tpu as pltpu
from jax.sharding import PartitionSpec as P

MESH = pl.DeviceIdType.MESH
F32 = jnp.float32
BF16 = jnp.bfloat16

ROWS, COLS = 32, 16
NZ = 8
IL, KL = 16, 32
N = 512
POS = IL * KL
C = 128


def layer_norm(values, axis):
    mean = jnp.mean(values, axis=axis, keepdims=True)
    centred = values - mean
    var = jnp.mean(centred * centred, axis=axis, keepdims=True)
    return centred * lax.rsqrt(var + 1e-05)


def sigmoid(x):
    return 0.5 * jnp.tanh(0.5 * x) + 0.5


def swap_blocks(v):
    v = list(v)
    lane = lax.broadcasted_iota(jnp.int32, v[0].shape, 1)
    apart, width = len(v) // 2, 64
    while apart:
        low = (lane % (2 * width)) < width
        for n in range(len(v)):
            if n % (2 * apart) < apart:
                x, y = v[n], v[n + apart]
                v[n] = jnp.where(low, x, pltpu.roll(y, width, 1))
                v[n + apart] = jnp.where(low, pltpu.roll(x, 128 - width, 1), y)
        apart, width = apart // 2, width // 2
    return v


def landed(ref, sem):
    pltpu.make_async_copy(ref, ref, sem).wait()


def kernel(
    pair_hbm, mask_hbm, w_hbm, gw_hbm, ow_hbm, out_ref,
    pair_ref, mask_ref, w_ref, gw_ref, ow_ref, proj, gate,
    send_l1, recv_l1, send_r1, recv_r1, turn_l, turn_r, send_l2, recv_l2, send_r2, recv_r2, turn_r2, right,
    send3, recv3, wide3, send4, recv4,
    met, load_sem, sl1, rl1, sr1, rr1, sl2, rl2, sr2, rr2, s3, r3, s4, r4,
):
    r, c = lax.axis_index("row"), lax.axis_index("col")
    xh, z, core = r // 16, (r // 2) % NZ, r % 2
    zc = r % 16

    def far(n):
        return 4 + (1 - 2 * (n % 2)) * ((n + 1) // 2)

    def col_peer(n):
        return (c // 8 + 1 - n % 2) % 2 * 8 + (c + far(n // 2)) % 8

    def zc_peer(n):
        return (z + far(n // 2)) % NZ * 2 + (core + 1 - n % 2) % 2

    def row(xh, z, core):
        return xh * 16 + z * 2 + core

    def send(src, dst, ssem, rsem, to_row, to_col):
        pltpu.make_async_remote_copy(src, dst, ssem, rsem, (to_row, to_col), MESH).start()

    loads = []
    for n, (src, dst) in enumerate(
        ((pair_hbm, pair_ref), (mask_hbm, mask_ref), (w_hbm, w_ref), (gw_hbm, gw_ref), (ow_hbm, ow_ref))
    ):
        loads.append(pltpu.make_async_copy(src, dst, load_sem.at[n]))
        loads[-1].start()

    barrier = pltpu.get_barrier_semaphore()

    def greet(to_row, to_col):
        pl.semaphore_signal(barrier, inc=1, device_id=(to_row, to_col), device_id_type=MESH)

    sibling, partner = r + 1 - 2 * core, (r + 16) % ROWS

    @pl.loop(1, COLS)
    def _(d):
        greet(r, (c + d) % COLS)

    @pl.loop(1, NZ)
    def _(d):
        greet(row(xh, (z + d) % NZ, core), c)

    greet(sibling, c)
    greet(partner, c)

    for load in loads[:2]:
        load.wait()

    normed = layer_norm(pair_ref[...].reshape(POS, C).astype(F32), 1)
    eye = lax.broadcasted_iota(jnp.int32, (KL, KL), 0) == lax.broadcasted_iota(jnp.int32, (KL, KL), 1)
    maskf = mask_ref[...].astype(F32)
    column = jnp.concatenate(
        [jnp.sum(jnp.where(eye, maskf[il : il + 1, :], 0.0), axis=1, keepdims=True) for il in range(IL)], axis=0
    )
    masked = (normed * column).astype(BF16)
    normed = normed.astype(BF16)
    loads[2].wait()
    full = lax.dot_general(w_ref[...], masked, (((0,), (1,)), ((), ())), preferred_element_type=F32)
    for t in range(4):
        proj[512 * t : 512 * t + 512, :] = full[:, 128 * t : 128 * t + 128]

    pl.semaphore_wait(barrier, 24)
    for to in (sibling, partner):
        pl.semaphore_signal(met, inc=1, device_id=(to, c), device_id_type=MESH)

    def left_of(g):
        x = []
        for t in range(4):
            at = [pl.ds(pl.multiple_of(512 * t + block * C + g * 8, 8), 8) for block in range(2)]
            x.append(sigmoid(proj[at[1], :]) * proj[at[0], :])
        x = [jnp.concatenate([x[n], x[n + 2]], axis=0) for n in range(2)]
        return jnp.concatenate(x, axis=1).astype(BF16)

    def right_of(e):
        x = []
        for t in range(4):
            at = [pl.ds(512 * t + block * C + e, 16, stride=8) for block in (2, 3)]
            x.append(sigmoid(proj[at[1], :]) * proj[at[0], :])
        return jnp.concatenate(x, axis=1).astype(BF16)

    def put_left1(n):
        g = col_peer(n)
        send_l1[g] = left_of(g)
        send(send_l1.at[g], recv_l1.at[c], sl1.at[g], rl1.at[c], r, g)

    @pl.loop(0, 7)
    def _(n):
        e = (z + far(n)) % NZ
        send_r1[e] = right_of(e)
        send(send_r1.at[e], recv_r1.at[z], sr1.at[e], rr1.at[z], row(xh, e, core), c)
        put_left1(2 * n)
        put_left1(2 * n + 1)

    put_left1(14)
    recv_r1[z] = right_of(z)
    recv_l1[c] = left_of(c)
    @pl.loop(0, 7)
    def _(n):
        e = (z + far(n)) % NZ
        landed(recv_r1.at[e], rr1.at[e])

    for t in range(4):
        turn_r[128 * t : 128 * t + 128, :] = recv_r1[:, :, 128 * t : 128 * t + 128].astype(F32).reshape(128, 128)
    for g in range(COLS):
        x = [turn_r[pl.ds(128 * t + g, 8, stride=16), :] for t in range(4)]
        for n in range(2):
            send_r2[g, :, 128 * n : 128 * n + 128] = jnp.concatenate([x[n], x[n + 2]], axis=0).astype(BF16)

    pl.semaphore_wait(met, 2)

    @pl.loop(0, 16)
    def _(n):
        g = col_peer(n + 1 - 2 * (n % 2))
        send(send_r2.at[g], recv_r2.at[xh * 16 + c], sr2.at[n], rr2.at[xh * 16 + c], partner, g)

    @pl.loop(0, 15)
    def _(n):
        g = col_peer(n)
        send(send_r2.at[g], recv_r2.at[xh * 16 + c], sr2.at[16 + n], rr2.at[xh * 16 + c], r, g)

    recv_r2[xh * 16 + c] = send_r2[c]

    @pl.loop(0, 15)
    def _(n):
        g = col_peer(n)
        landed(recv_l1.at[g], rl1.at[g])

    for a in range(4):
        for b in range(2):
            tiles = [recv_l1[4 * a + q, :, 128 * b : 128 * b + 128].astype(F32) for q in range(4)]
            for q, tile in enumerate(swap_blocks(tiles)):
                at = 128 * a + 16 * (4 * b + q)
                turn_l[at : at + 16, :] = tile
    for e in range(NZ):
        for a in range(4):
            x = [turn_l[pl.ds(128 * a + 8 * h + e, 8, stride=16), :] for h in range(2)]
            send_l2[e, :, 128 * a : 128 * a + 128] = jnp.concatenate(x, axis=0).astype(BF16)

    @pl.loop(0, 7)
    def _(n):
        e = (z + far(n)) % NZ
        send(send_l2.at[e], recv_l2.at[zc], sl2.at[n], rl2.at[zc], row(xh, e, core), c)

    recv_l2[zc] = send_l2[z]
    send(send_l2.at[z], recv_l2.at[zc], sl2.at[7], rl2.at[zc], sibling, c)

    def pass_right(i):
        m = xh * 16 + col_peer(14 - i)
        landed(recv_r2.at[m], rr2.at[m])
        send(recv_r2.at[m], recv_r2.at[m], sr2.at[18 + i], rr2.at[m], partner, c)

    def pass_left(i):
        m = (z + far(6 - i)) % NZ * 2 + core
        landed(recv_l2.at[m], rl2.at[m])
        send(recv_l2.at[m], recv_l2.at[m], sl2.at[8 + i], rl2.at[m], sibling, c)

    @pl.loop(0, 6)
    def _(i):
        pass_left(i)

    pass_left(6)

    loads[3].wait()
    loads[4].wait()
    gate[...] = sigmoid(jnp.dot(normed, gw_ref[...], preferred_element_type=F32)).reshape(IL, KL, C)

    for h in range(2):

        @pl.loop(16 * h, 16 * h + 16)
        def _(m):
            @pl.when(m != xh * 16 + c)
            def _():
                landed(recv_r2.at[m], rr2.at[m])

        for a in range(4):
            for b in range(2):
                tiles = [recv_r2[16 * h + 4 * a + q, :, 128 * b : 128 * b + 128].astype(F32) for q in range(4)]
                for q, tile in enumerate(swap_blocks(tiles)):
                    at = 256 * a + 128 * h + 16 * (4 * b + q)
                    turn_r2[at : at + 16, :] = tile
        for m in range(NZ):
            for a in range(4):
                x = [turn_r2[pl.ds(256 * a + 128 * h + 8 * jh + m, 8, stride=16), :] for jh in range(2)]
                at = 128 * h + 16 * m
                right[at : at + 16, 128 * a : 128 * a + 128] = jnp.concatenate(x, axis=0).astype(BF16)

    @pl.loop(0, NZ)
    def _(e):
        m = 2 * e + 1 - core
        landed(recv_l2.at[m], rl2.at[m])

    tri = lax.dot_general(
        recv_l2[...].reshape(256, N), right[...], (((1,), (1,)), ((), ())), preferred_element_type=F32
    )
    send3[...] = tri.astype(BF16).reshape(16, IL, 256)

    @pl.loop(0, 15)
    def _(n):
        to = (z + far(n % 8)) % NZ * 2 + (core + 1 - n // 8) % 2
        send(send3.at[to], recv3.at[zc], s3.at[to], r3.at[zc], xh * 16 + to, c)

    recv3[zc] = send3[zc]

    @pl.loop(0, 15)
    def _(n):
        m = zc_peer(n)
        landed(recv3.at[m], r3.at[m])

    for a in range(2):
        wide3[256 * a : 256 * a + 256, :] = recv3[:, :, 128 * a : 128 * a + 128].astype(F32).reshape(256, 128)
    for a in range(2):
        for k in range(2):
            parts = []
            for h in range(2):
                at = 256 * a + 16 * k + 8 * h
                parts.append(swap_blocks([wide3[pl.ds(at + q, 8, stride=32), :] for q in range(8)]))
            for q in range(8):
                send4[8 * a + q, :, 128 * k : 128 * k + 128] = jnp.concatenate(
                    [parts[0][q], parts[1][q]], axis=0
                ).astype(BF16)

    @pl.loop(0, 15)
    def _(n):
        g = col_peer(n)
        send(send4.at[g], recv4.at[c], s4.at[g], r4.at[c], r, g)

    recv4[c] = send4[c]

    @pl.loop(0, 15)
    def _(n):
        g = col_peer(n)
        landed(recv4.at[g], r4.at[g])

    got = recv4[...].astype(F32)
    for h in range(2):
        tnorm = layer_norm(got[:, 8 * h : 8 * h + 8, :].reshape(C, 256), 0).astype(BF16)
        prod = lax.dot_general(tnorm, ow_ref[...], (((0,), (0,)), ((), ())), preferred_element_type=F32)
        for k in range(2):
            part = prod[128 * k : 128 * k + 128, :].reshape(8, 16, C)
            update = gate[8 * h : 8 * h + 8, 16 * k : 16 * k + 16, :] * part
            out_ref[8 * h : 8 * h + 8, 16 * k : 16 * k + 16, :] = update.astype(BF16)

    @pl.loop(0, 15)
    def _(n):
        g, m = col_peer(n), zc_peer(n)
        landed(send_l1.at[g], sl1.at[g])
        landed(send_l2.at[0], sl2.at[n])
        landed(send3.at[m], s3.at[m])
        landed(send4.at[g], s4.at[g])

    @pl.loop(0, 7)
    def _(n):
        e = (z + far(n)) % NZ
        landed(send_r1.at[e], sr1.at[e])

    @pl.loop(0, 31)
    def _(n):
        landed(send_r2.at[0], sr2.at[n])


def body(pair, pair_mask, in_weights, gate_weight, out_weight):
    dma = pltpu.SemaphoreType.DMA
    vmem = pltpu.VMEM
    return pl.pallas_call(
        kernel,
        out_shape=jax.ShapeDtypeStruct((IL, KL, C), BF16),
        in_specs=[pl.BlockSpec(memory_space=pl.ANY)] * 5,
        out_specs=pl.BlockSpec(memory_space=vmem),
        scratch_shapes=[
            vmem((IL, KL, C), BF16),
            vmem((IL, KL), jnp.int32),
            vmem((C, 4 * C), BF16),
            vmem((C, C), BF16),
            vmem((C, C), BF16),
            vmem((4 * 512, 128), F32),
            vmem((IL, KL, C), F32),
            vmem((COLS, 16, 256), BF16),
            vmem((COLS, 16, 256), BF16),
            vmem((NZ, 16, POS), BF16),
            vmem((NZ, 16, POS), BF16),
            vmem((4 * 128, 128), F32),
            vmem((4 * 128, 128), F32),
            vmem((NZ, 16, N), BF16),
            vmem((16, 16, N), BF16),
            vmem((COLS, 16, 256), BF16),
            vmem((2 * COLS, 16, 256), BF16),
            vmem((4 * 256, 128), F32),
            vmem((256, N), BF16),
            vmem((16, IL, 256), BF16),
            vmem((16, IL, 256), BF16),
            vmem((2 * 256, 128), F32),
            vmem((COLS, 16, 256), BF16),
            vmem((COLS, 16, 256), BF16),
            pltpu.SemaphoreType.REGULAR,
            dma((5,)),
            dma((16,)),
            dma((16,)),
            dma((8,)),
            dma((8,)),
            dma((16,)),
            dma((16,)),
            dma((32,)),
            dma((32,)),
            dma((16,)),
            dma((16,)),
            dma((16,)),
            dma((16,)),
        ],
        compiler_params=pltpu.CompilerParams(
            collective_id=0, has_side_effects=True, vmem_limit_bytes=58 * 1024 * 1024
        ),
        cost_estimate=pl.CostEstimate(flops=170_000_000, bytes_accessed=500_000, transcendentals=200_000),
    )(pair, pair_mask, in_weights, gate_weight, out_weight)


def solution(mesh):
    in_specs = (P("row", "col", None), P("row", "col"), P(), P(), P())
    out_specs = P("row", "col", None)
    return jax.shard_map(body, mesh=mesh, in_specs=in_specs, out_specs=out_specs, check_vma=False)
```

```python
import jax
import jax.numpy as jnp
from jax import lax
from jax.experimental import pallas as pl
from jax.experimental.pallas import tpu as pltpu
from jax.sharding import PartitionSpec as P

MESH = pl.DeviceIdType.MESH
F32 = jnp.float32
BF16 = jnp.bfloat16

ROWS, COLS = 32, 16
NZ = 8
IL, KL = 16, 32
N = 512
POS = IL * KL
C = 128


def layer_norm(values, axis):
    mean = jnp.mean(values, axis=axis, keepdims=True)
    centred = values - mean
    var = jnp.mean(centred * centred, axis=axis, keepdims=True)
    return centred * lax.rsqrt(var + 1e-05)


def sigmoid(x):
    return 0.5 * jnp.tanh(0.5 * x) + 0.5


def swap_blocks(v):
    v = list(v)
    lane = lax.broadcasted_iota(jnp.int32, v[0].shape, 1)
    apart, width = len(v) // 2, 64
    while apart:
        low = (lane % (2 * width)) < width
        for n in range(len(v)):
            if n % (2 * apart) < apart:
                x, y = v[n], v[n + apart]
                v[n] = jnp.where(low, x, pltpu.roll(y, width, 1))
                v[n + apart] = jnp.where(low, pltpu.roll(x, 128 - width, 1), y)
        apart, width = apart // 2, width // 2
    return v


def landed(ref, sem):
    pltpu.make_async_copy(ref, ref, sem).wait()


def kernel(
    pair_hbm, mask_hbm, w_hbm, gw_hbm, ow_hbm, out_ref,
    pair_ref, mask_ref, w_ref, gw_ref, ow_ref, proj, gate,
    send_l1, recv_l1, send_r1, recv_r1, turn_l, turn_r, send_l2, recv_l2, send_r2, recv_r2, turn_r2, right,
    send3, recv3, wide3, send4, recv4,
    met, load_sem, sl1, rl1, sr1, rr1, sl2, rl2, sr2, rr2, s3, r3, s4, r4,
):
    r, c = lax.axis_index("row"), lax.axis_index("col")
    xh, z, core = r // 16, (r // 2) % NZ, r % 2
    zc = r % 16

    def far(n):
        return 4 + (1 - 2 * (n % 2)) * ((n + 1) // 2)

    def col_peer(n):
        return (c // 8 + 1 - n % 2) % 2 * 8 + (c + far(n // 2)) % 8

    def zc_peer(n):
        return (z + far(n // 2)) % NZ * 2 + (core + 1 - n % 2) % 2

    def row(xh, z, core):
        return xh * 16 + z * 2 + core

    def send(src, dst, ssem, rsem, to_row, to_col):
        pltpu.make_async_remote_copy(src, dst, ssem, rsem, (to_row, to_col), MESH).start()

    barrier = pltpu.get_barrier_semaphore()

    def greet(to_row, to_col):
        pl.semaphore_signal(barrier, inc=1, device_id=(to_row, to_col), device_id_type=MESH)

    sibling, partner = r + 1 - 2 * core, (r + 16) % ROWS

    @pl.loop(1, COLS)
    def _(d):
        greet(r, (c + d) % COLS)

    @pl.loop(1, NZ)
    def _(d):
        greet(row(xh, (z + d) % NZ, core), c)

    greet(sibling, c)
    greet(partner, c)

    loads = []
    for n, (src, dst) in enumerate(
        ((pair_hbm, pair_ref), (mask_hbm, mask_ref), (w_hbm, w_ref), (gw_hbm, gw_ref), (ow_hbm, ow_ref))
    ):
        loads.append(pltpu.make_async_copy(src, dst, load_sem.at[n]))
        loads[-1].start()

    for load in loads[:2]:
        load.wait()

    normed = layer_norm(pair_ref[...].reshape(POS, C).astype(F32), 1)
    eye = lax.broadcasted_iota(jnp.int32, (KL, KL), 0) == lax.broadcasted_iota(jnp.int32, (KL, KL), 1)
    maskf = mask_ref[...].astype(F32)
    column = jnp.concatenate(
        [jnp.sum(jnp.where(eye, maskf[il : il + 1, :], 0.0), axis=1, keepdims=True) for il in range(IL)], axis=0
    )
    masked = (normed * column).astype(BF16)
    normed = normed.astype(BF16)
    loads[2].wait()
    full = lax.dot_general(w_ref[...], masked, (((0,), (1,)), ((), ())), preferred_element_type=F32)
    for t in range(4):
        proj[512 * t : 512 * t + 512, :] = full[:, 128 * t : 128 * t + 128]

    pl.semaphore_wait(barrier, 24)
    for to in (sibling, partner):
        pl.semaphore_signal(met, inc=1, device_id=(to, c), device_id_type=MESH)

    def left_of(g):
        x = []
        for t in range(4):
            at = [pl.ds(pl.multiple_of(512 * t + block * C + g * 8, 8), 8) for block in range(2)]
            x.append(sigmoid(proj[at[1], :]) * proj[at[0], :])
        x = [jnp.concatenate([x[n], x[n + 2]], axis=0) for n in range(2)]
        return jnp.concatenate(x, axis=1).astype(BF16)

    def right_of(e):
        x = []
        for t in range(4):
            at = [pl.ds(512 * t + block * C + e, 16, stride=8) for block in (2, 3)]
            x.append(sigmoid(proj[at[1], :]) * proj[at[0], :])
        return jnp.concatenate(x, axis=1).astype(BF16)

    def put_left1(n):
        g = col_peer(n)
        send_l1[g] = left_of(g)
        send(send_l1.at[g], recv_l1.at[c], sl1.at[g], rl1.at[c], r, g)

    @pl.loop(0, 7)
    def _(n):
        e = (z + far(n)) % NZ
        send_r1[e] = right_of(e)
        send(send_r1.at[e], recv_r1.at[z], sr1.at[e], rr1.at[z], row(xh, e, core), c)
        put_left1(2 * n)
        put_left1(2 * n + 1)

    put_left1(14)
    recv_r1[z] = right_of(z)
    recv_l1[c] = left_of(c)
    @pl.loop(0, 7)
    def _(n):
        e = (z + far(n)) % NZ
        landed(recv_r1.at[e], rr1.at[e])

    for t in range(4):
        turn_r[128 * t : 128 * t + 128, :] = recv_r1[:, :, 128 * t : 128 * t + 128].astype(F32).reshape(128, 128)
    for g in range(COLS):
        x = [turn_r[pl.ds(128 * t + g, 8, stride=16), :] for t in range(4)]
        for n in range(2):
            send_r2[g, :, 128 * n : 128 * n + 128] = jnp.concatenate([x[n], x[n + 2]], axis=0).astype(BF16)

    pl.semaphore_wait(met, 2)

    @pl.loop(0, 16)
    def _(n):
        g = col_peer(n + 1 - 2 * (n % 2))
        send(send_r2.at[g], recv_r2.at[xh * 16 + c], sr2.at[n], rr2.at[xh * 16 + c], partner, g)

    @pl.loop(0, 15)
    def _(n):
        g = col_peer(n)
        send(send_r2.at[g], recv_r2.at[xh * 16 + c], sr2.at[16 + n], rr2.at[xh * 16 + c], r, g)

    recv_r2[xh * 16 + c] = send_r2[c]

    @pl.loop(0, 15)
    def _(n):
        g = col_peer(n)
        landed(recv_l1.at[g], rl1.at[g])

    for a in range(4):
        for b in range(2):
            tiles = [recv_l1[4 * a + q, :, 128 * b : 128 * b + 128].astype(F32) for q in range(4)]
            for q, tile in enumerate(swap_blocks(tiles)):
                at = 128 * a + 16 * (4 * b + q)
                turn_l[at : at + 16, :] = tile
    for e in range(NZ):
        for a in range(4):
            x = [turn_l[pl.ds(128 * a + 8 * h + e, 8, stride=16), :] for h in range(2)]
            send_l2[e, :, 128 * a : 128 * a + 128] = jnp.concatenate(x, axis=0).astype(BF16)

    @pl.loop(0, 7)
    def _(n):
        e = (z + far(n)) % NZ
        send(send_l2.at[e], recv_l2.at[zc], sl2.at[n], rl2.at[zc], row(xh, e, core), c)

    recv_l2[zc] = send_l2[z]
    send(send_l2.at[z], recv_l2.at[zc], sl2.at[7], rl2.at[zc], sibling, c)

    def pass_right(i):
        m = xh * 16 + col_peer(14 - i)
        landed(recv_r2.at[m], rr2.at[m])
        send(recv_r2.at[m], recv_r2.at[m], sr2.at[18 + i], rr2.at[m], partner, c)

    def pass_left(i):
        m = (z + far(6 - i)) % NZ * 2 + core
        landed(recv_l2.at[m], rl2.at[m])
        send(recv_l2.at[m], recv_l2.at[m], sl2.at[8 + i], rl2.at[m], sibling, c)

    @pl.loop(0, 6)
    def _(i):
        pass_left(i)

    pass_left(6)

    loads[3].wait()
    loads[4].wait()
    gate[...] = sigmoid(jnp.dot(normed, gw_ref[...], preferred_element_type=F32)).reshape(IL, KL, C)

    for h in range(2):

        @pl.loop(16 * h, 16 * h + 16)
        def _(m):
            @pl.when(m != xh * 16 + c)
            def _():
                landed(recv_r2.at[m], rr2.at[m])

        for a in range(4):
            for b in range(2):
                tiles = [recv_r2[16 * h + 4 * a + q, :, 128 * b : 128 * b + 128].astype(F32) for q in range(4)]
                for q, tile in enumerate(swap_blocks(tiles)):
                    at = 256 * a + 128 * h + 16 * (4 * b + q)
                    turn_r2[at : at + 16, :] = tile
        for m in range(NZ):
            for a in range(4):
                x = [turn_r2[pl.ds(256 * a + 128 * h + 8 * jh + m, 8, stride=16), :] for jh in range(2)]
                at = 128 * h + 16 * m
                right[at : at + 16, 128 * a : 128 * a + 128] = jnp.concatenate(x, axis=0).astype(BF16)

    @pl.loop(0, NZ)
    def _(e):
        m = 2 * e + 1 - core
        landed(recv_l2.at[m], rl2.at[m])

    tri = lax.dot_general(
        recv_l2[...].reshape(256, N), right[...], (((1,), (1,)), ((), ())), preferred_element_type=F32
    )
    send3[...] = tri.astype(BF16).reshape(16, IL, 256)

    @pl.loop(0, 15)
    def _(n):
        to = zc_peer(n)
        send(send3.at[to], recv3.at[zc], s3.at[to], r3.at[zc], xh * 16 + to, c)

    recv3[zc] = send3[zc]

    @pl.loop(0, 15)
    def _(n):
        m = zc_peer(n)
        landed(recv3.at[m], r3.at[m])

    for a in range(2):
        wide3[256 * a : 256 * a + 256, :] = recv3[:, :, 128 * a : 128 * a + 128].astype(F32).reshape(256, 128)
    for a in range(2):
        for k in range(2):
            parts = []
            for h in range(2):
                at = 256 * a + 16 * k + 8 * h
                parts.append(swap_blocks([wide3[pl.ds(at + q, 8, stride=32), :] for q in range(8)]))
            for q in range(8):
                send4[8 * a + q, :, 128 * k : 128 * k + 128] = jnp.concatenate(
                    [parts[0][q], parts[1][q]], axis=0
                ).astype(BF16)

    @pl.loop(0, 15)
    def _(n):
        g = col_peer(n)
        send(send4.at[g], recv4.at[c], s4.at[g], r4.at[c], r, g)

    recv4[c] = send4[c]

    @pl.loop(0, 15)
    def _(n):
        g = col_peer(n)
        landed(recv4.at[g], r4.at[g])

    got = recv4[...].astype(F32)
    for h in range(2):
        tnorm = layer_norm(got[:, 8 * h : 8 * h + 8, :].reshape(C, 256), 0).astype(BF16)
        prod = lax.dot_general(tnorm, ow_ref[...], (((0,), (0,)), ((), ())), preferred_element_type=F32)
        for k in range(2):
            part = prod[128 * k : 128 * k + 128, :].reshape(8, 16, C)
            update = gate[8 * h : 8 * h + 8, 16 * k : 16 * k + 16, :] * part
            out_ref[8 * h : 8 * h + 8, 16 * k : 16 * k + 16, :] = update.astype(BF16)

    @pl.loop(0, 15)
    def _(n):
        g, m = col_peer(n), zc_peer(n)
        landed(send_l1.at[g], sl1.at[g])
        landed(send_l2.at[0], sl2.at[n])
        landed(send3.at[m], s3.at[m])
        landed(send4.at[g], s4.at[g])

    @pl.loop(0, 7)
    def _(n):
        e = (z + far(n)) % NZ
        landed(send_r1.at[e], sr1.at[e])

    @pl.loop(0, 31)
    def _(n):
        landed(send_r2.at[0], sr2.at[n])


def body(pair, pair_mask, in_weights, gate_weight, out_weight):
    dma = pltpu.SemaphoreType.DMA
    vmem = pltpu.VMEM
    return pl.pallas_call(
        kernel,
        out_shape=jax.ShapeDtypeStruct((IL, KL, C), BF16),
        in_specs=[pl.BlockSpec(memory_space=pl.ANY)] * 5,
        out_specs=pl.BlockSpec(memory_space=vmem),
        scratch_shapes=[
            vmem((IL, KL, C), BF16),
            vmem((IL, KL), jnp.int32),
            vmem((C, 4 * C), BF16),
            vmem((C, C), BF16),
            vmem((C, C), BF16),
            vmem((4 * 512, 128), F32),
            vmem((IL, KL, C), F32),
            vmem((COLS, 16, 256), BF16),
            vmem((COLS, 16, 256), BF16),
            vmem((NZ, 16, POS), BF16),
            vmem((NZ, 16, POS), BF16),
            vmem((4 * 128, 128), F32),
            vmem((4 * 128, 128), F32),
            vmem((NZ, 16, N), BF16),
            vmem((16, 16, N), BF16),
            vmem((COLS, 16, 256), BF16),
            vmem((2 * COLS, 16, 256), BF16),
            vmem((4 * 256, 128), F32),
            vmem((256, N), BF16),
            vmem((16, IL, 256), BF16),
            vmem((16, IL, 256), BF16),
            vmem((2 * 256, 128), F32),
            vmem((COLS, 16, 256), BF16),
            vmem((COLS, 16, 256), BF16),
            pltpu.SemaphoreType.REGULAR,
            dma((5,)),
            dma((16,)),
            dma((16,)),
            dma((8,)),
            dma((8,)),
            dma((16,)),
            dma((16,)),
            dma((32,)),
            dma((32,)),
            dma((16,)),
            dma((16,)),
            dma((16,)),
            dma((16,)),
        ],
        compiler_params=pltpu.CompilerParams(
            collective_id=0, has_side_effects=True, vmem_limit_bytes=58 * 1024 * 1024
        ),
        cost_estimate=pl.CostEstimate(flops=170_000_000, bytes_accessed=500_000, transcendentals=200_000),
    )(pair, pair_mask, in_weights, gate_weight, out_weight)


def solution(mesh):
    in_specs = (P("row", "col", None), P("row", "col"), P(), P(), P())
    out_specs = P("row", "col", None)
    return jax.shard_map(body, mesh=mesh, in_specs=in_specs, out_specs=out_specs, check_vma=False)
```
